512 devices in a mesh: tile: 64 (over x, z, core), dp: 8 (over y).
Axes of the slice: x: 4, y: 8, z: 8, core: 2. Of those that a mesh axis runs over, the one named last changes fastest.
Arguments:
- tile_ids: int32 [524288, 1], P(('tile', 'dp')), may hold values from 0 to 63; in each aligned block of 1024 rows (0 to 1023, 1024 to 2047, ...) at most 64 rows name the same one
- corners: int32 [2, 524288], P(None, ('tile', 'dp')), may hold values from 0 to 62
- offsets: float32 [2, 524288], P(None, ('tile', 'dp')), may hold values from 0 to 1
- targets: float32 [3, 32768], P(None, ('tile', 'dp')), may hold values from 0 to 1
- grid: bfloat16 [256, 262144], P('dp', 'tile'), may hold values from -6 to 6
- w_first: bfloat16 [256, 512], replicated, may hold values from -0.375 to 0.375
- w_second: bfloat16 [512, 4], replicated, may hold values from -0.25 to 0.25
Outputs:
- grid_grad: float32 [256, 262144], P('dp', 'tile')
- grad_first: float32 [256, 512], replicated
- grad_second: float32 [512, 4], replicated
The draws below stay inside these ranges and needn't reach their ends.
Inputs may be any that keep to these rules, and one draw needn't show every extreme that they name: `tile_ids`: among the samples of one device (aligned blocks of 1024 rows) at most 64 name the same tile; in some blocks one tile is named by exactly 64.
All inputs are finite; a program needn't handle non-finite values.
Results may differ from the reference program's by a relative error of at most 0.0041.
The reference program's roundings to bfloat16 on the way (of `corner_weights`, `features`, `hidden`, `pre_grad` and `feature_grad`) count: a program that leaves them out, or rounds other values in their place, can miss the bound.
Values may be sent and summed in bfloat16 or wider, within the bound.
No kernel may reach another device: no remote copies, remote signals or barrier semaphores. Data moves between devices by JAX's collectives and lax.ppermute only.
A program may use at most 192 MiB of HBM per device.

```python
import math
import jax
import jax.numpy as jnp
import numpy as np
from jax import lax

C = 256
HID = 512
GSIDE = 64
MARCH = 15
RAYS_DEV = 64
SAMP_DEV = 1024
CAP = 64
TILES = 64
SAMPLES = 524288
RAYS = 32768


def set_ends(values, key, least, high):
    longest = values.shape.index(max(values.shape))
    spots = []
    for shift in (0, 1):
        where = [jax.random.randint(jax.random.fold_in(key, axis), (), 0, length) for axis, length in enumerate(values.shape)]
        where[longest] = (where[longest] + shift) % values.shape[longest]
        spots.append(tuple(where))
    return values.at[spots[0]].set(least).at[spots[1]].set(high)


def block_scale(own_key, dims, cuts, least, largest):
    loudness = 1.0
    for position, parts in cuts:
        draws = jax.random.uniform(jax.random.fold_in(jax.random.fold_in(own_key, 6), position), (parts,), jnp.float32, least / len(cuts), largest / len(cuts))
        loudness = loudness * jnp.repeat(jnp.exp(draws), dims[position] // parts).reshape((-1,) + (1,) * (len(dims) - 1 - position))
    return loudness


def deal_out(key, own, number, rows, number_of, top, bound, slope):
    order = jax.random.permutation(key, number_of)
    crowded, ordinary = portions_of(number_of, rows * top, bound, slope, True), portions_of(number_of, rows * top, bound, slope, False)
    places = jnp.arange(number_of)

    def named(tallies, rotation):
        used = int((tallies > 0).sum())
        fixed = max(1, used // 4)
        passed = fixed + (places - fixed + rotation * (used - fixed)) % max(1, number_of - fixed)
        return jnp.zeros((number_of,), jnp.int32).at[order[jnp.where(places < fixed, places, passed)]].set(jnp.asarray(tallies, jnp.int32))

    tallies = jnp.where(number % 4 == 0, named(crowded, number // 4), named(ordinary, number - number // 4 - 1))
    mixed = jax.random.permutation(jax.random.fold_in(own, 3), number_of)
    donor, sink = mixed[0:number_of // 2 * 2:2], mixed[1:number_of // 2 * 2:2]
    room = jnp.minimum(tallies[donor] - 1, bound - tallies[sink]) // 2
    room = jnp.where((donor == order[0]) | (sink == order[0]) | (tallies[sink] == 0), 0, jnp.maximum(room, 0))
    passed = jax.random.randint(jax.random.fold_in(own, 4), (number_of // 2,), 0, 1 << 20) % (room + 1)
    tallies = tallies.at[donor].add(-passed).at[sink].add(passed)
    items = jnp.searchsorted(jnp.cumsum(tallies), jnp.arange(rows * top), side="right").astype(jnp.int32)
    listing = items.reshape(top, rows).T
    listing = listing[jax.random.permutation(jax.random.fold_in(own, 1), rows)]
    rotation = jax.random.randint(jax.random.fold_in(own, 2), (rows, 1), 0, top)
    return jnp.take_along_axis(listing, (jnp.arange(top)[None, :] + rotation) % top, axis=1)


def portions_of(amount, total, most, skew, full):
    loads = [(1 << 20) // math.isqrt(standing ** skew) + 1 for standing in range(1, amount + 1)]
    largest = most if full else min(most, max(-(-total // amount), total * loads[0] // sum(loads)))
    least = 1 if total - largest >= amount - 1 else 0
    holding, spare = [largest] + [least] * (amount - 1), total - largest - least * (amount - 1)
    while spare > 0:
        movable = [i for i in range(1, amount) if holding[i] < largest] or [i for i in range(1, amount) if holding[i] < most]
        mass, remaining = sum([loads[i] for i in movable]), spare
        for i in movable:
            addition = min(most - holding[i], max(1, remaining * loads[i] // mass), spare)
            holding[i] = holding[i] + addition
            spare = spare - addition
    return np.array(holding)


def bell_draw(key, dims, width, most, pieces=(), kind=jnp.bfloat16):
    values = width * jax.random.normal(key, dims, jnp.float32)
    if pieces:
        values = values * block_scale(key, dims, pieces, -0.22, 0.18)
    return jnp.clip(values, -most, most).astype(kind)


def setup_inputs(seed: int = 0) -> dict:
    seeds = jax.random.split(jax.random.key(seed), 8)
    tile_ids_keys = jax.random.split(jax.random.fold_in(seeds[0], 1), SAMPLES // SAMP_DEV)
    tile_ids_turns = jax.random.permutation(jax.random.fold_in(seeds[0], 3), SAMPLES // SAMP_DEV)
    tile_ids = jax.vmap(lambda own, number: deal_out(jax.random.fold_in(seeds[0], 2), own, number, SAMP_DEV, TILES, 1, CAP, 2))(tile_ids_keys, tile_ids_turns).reshape((SAMPLES, 1))
    corners = set_ends(jax.random.randint(seeds[1], (2, SAMPLES), 0, GSIDE - 1), jax.random.fold_in(seeds[1], 1), 0, (GSIDE - 1) - 1).astype(jnp.int32)
    offsets = jnp.clip(1.0 * jax.random.uniform(seeds[2], (2, SAMPLES), jnp.float32) ** block_scale(seeds[2], (2, SAMPLES), ((1, 512),), -0.2, 0.2), 0.0, 1.0)
    targets = jnp.clip(1.0 * jax.random.uniform(seeds[3], (3, RAYS), jnp.float32) ** block_scale(seeds[3], (3, RAYS), ((1, 512),), -0.2, 0.2), 0.0, 1.0)
    grid = bell_draw(seeds[4], (C, TILES * GSIDE * GSIDE), 1.0, 6.0, ((0, 8), (1, 64)))
    w_first = bell_draw(seeds[5], (C, HID), C ** -0.5, 0.375)
    w_second = bell_draw(seeds[6], (HID, 4), HID ** -0.5, 0.25)
    return dict(tile_ids=tile_ids, corners=corners, offsets=offsets, targets=targets, grid=grid, w_first=w_first, w_second=w_second)


march_step = 0.1
ambient = 0.3


def corner_weights(offsets):
    along = offsets[0]
    across = offsets[1]
    stacked = jnp.stack([(1.0 - along) * (1.0 - across), (1.0 - along) * across, along * (1.0 - across), along * across])
    return stacked.astype(jnp.bfloat16)


def shade_grads(features, w_first, w_second, wanted):
    pre_act = jnp.dot(features, w_first, preferred_element_type=jnp.float32)
    hidden = jax.nn.silu(pre_act).astype(jnp.bfloat16)
    decoded = jnp.dot(hidden, w_second, preferred_element_type=jnp.float32)
    ray_count = wanted.shape[1]
    decoded = decoded.reshape(ray_count, MARCH + 1, 4)
    raw_density = decoded[:, 1:, 0]
    density = jax.nn.softplus(raw_density)
    transmit = jnp.exp(-march_step * jnp.sum(density, axis=1))
    albedo = jax.nn.sigmoid(decoded[:, 0, 1:])
    lighting = ambient + (1.0 - ambient) * transmit
    errors = albedo * lighting[:, None] - wanted.T
    albedo_grad = errors * lighting[:, None]
    transmit_grad = (1.0 - ambient) * jnp.sum(errors * albedo, axis=1)
    march_grad = (-march_step * transmit * transmit_grad)[:, None] * jax.nn.sigmoid(raw_density)
    surface_grad = jnp.concatenate([jnp.zeros((ray_count, 1), jnp.float32), albedo_grad * albedo * (1.0 - albedo)], axis=1)
    sun_grad = jnp.concatenate([march_grad[:, :, None], jnp.zeros((ray_count, MARCH, 3), jnp.float32)], axis=2)
    decoded_grad = jnp.concatenate([surface_grad[:, None, :], sun_grad], axis=1).reshape(-1, 4)
    grad_second = jnp.dot(hidden.astype(jnp.float32).T, decoded_grad, precision=lax.Precision.HIGHEST)
    hidden_grad = jnp.dot(decoded_grad, w_second.astype(jnp.float32).T, precision=lax.Precision.HIGHEST)
    smooth_gate = jax.nn.sigmoid(pre_act)
    pre_grad = (hidden_grad * smooth_gate * (1.0 + pre_act * (1.0 - smooth_gate))).astype(jnp.bfloat16)
    grad_first = lax.dot_general(features, pre_grad, (((0,), (0,)), ((), ())), preferred_element_type=jnp.float32)
    feature_grad = lax.dot_general(pre_grad, w_first, (((1,), (1,)), ((), ())), preferred_element_type=jnp.float32)
    return grad_first, grad_second, feature_grad.astype(jnp.bfloat16)


def reference(tile_ids, corners, offsets, targets, grid, w_first, w_second):
    cell_count = GSIDE * GSIDE
    blocks = tile_ids.shape[0] // SAMP_DEV
    base_cell = (tile_ids[:, 0] * cell_count + corners[0] * GSIDE + corners[1]).astype(jnp.int32)
    global_cells = base_cell.reshape(blocks, SAMP_DEV)
    weights = corner_weights(offsets).reshape(4, blocks, SAMP_DEV).transpose(1, 0, 2)
    wanted = targets.reshape(3, blocks, RAYS_DEV).transpose(1, 0, 2)
    corner_shift = jnp.array([0, 1, GSIDE, GSIDE + 1], dtype=jnp.int32)

    def one_block(totals, block_item):
        grid_total, first_total, second_total = totals
        cells_here, weights_here, wanted_here = block_item
        corner_cells = (cells_here[None, :] + corner_shift[:, None]).astype(jnp.int32)
        corner_rows = grid[:, corner_cells].astype(jnp.float32)
        features = jnp.einsum("cks,ks->sc", corner_rows, weights_here.astype(jnp.float32), precision=lax.Precision.HIGHEST).astype(jnp.bfloat16)
        grad_first, grad_second, feature_grad = shade_grads(features, w_first, w_second, wanted_here)
        spread_terms = weights_here.astype(jnp.float32)[None, :, :] * feature_grad.astype(jnp.float32).T[:, None, :]
        grid_total = grid_total.at[:, corner_cells].add(spread_terms)
        return (grid_total, first_total + grad_first, second_total + grad_second), None

    start = (jnp.zeros(grid.shape, jnp.float32), jnp.zeros(w_first.shape, jnp.float32), jnp.zeros(w_second.shape, jnp.float32))
    totals, unused = lax.scan(one_block, start, (global_cells, weights, wanted))
    return totals[0], totals[1], totals[2]
```

```python
import functools

import jax
import jax.numpy as jnp
from jax import lax
from jax.experimental import pallas as pl
from jax.experimental.pallas import tpu as pltpu
from jax.sharding import PartitionSpec as P

GSIDE = 64
MARCH = 15
march_step = 0.1
ambient = 0.3

bf16 = jnp.bfloat16
f32 = jnp.float32
HIGHEST = lax.Precision.HIGHEST
FIELDS = 6
VMEM_BYTES = 56 << 20


def matmul(a, b, dims=((1,), (0,)), precision=None):
    return lax.dot_general(a, b, (dims, ((), ())), precision=precision, preferred_element_type=f32)


def row_iota(shape, dim):
    return lax.broadcasted_iota(jnp.int32, shape, dim)


def slot_kernel(tile_ref, corners_ref, offsets_ref, send_ref, rank_ref, *, tiles, capacity):
    tile = tile_ref[...]
    samples = tile.shape[1]
    members = row_iota((tiles, samples), 0) == tile
    member_rows = members.astype(f32).astype(bf16)
    before = (
        row_iota((samples, samples), 0) < row_iota((samples, samples), 1)
    ).astype(f32).astype(bf16)
    earlier = matmul(member_rows, before)
    rank = jnp.sum(jnp.where(members, earlier, 0.0), axis=0, keepdims=True)
    rank_ref[...] = rank
    at_rank = row_iota((capacity, samples), 0) == rank.astype(jnp.int32)
    along = offsets_ref[0:1]
    across = offsets_ref[1:2]
    fields = [
        corners_ref[0:1].astype(f32),
        corners_ref[1:2].astype(f32),
        (1.0 - along) * (1.0 - across),
        (1.0 - along) * across,
        along * (1.0 - across),
        along * across,
    ]
    for number, field in enumerate(fields):
        placed = jnp.where(at_rank, field, 0.0).astype(bf16)
        send_ref[number] = matmul(member_rows, placed, ((1,), (1,))).astype(bf16)


def sample_columns(info):
    slots = info.shape[1]
    col = row_iota((GSIDE, slots), 0).astype(f32).astype(bf16)

    def full(number):
        return jnp.broadcast_to(info[number : number + 1], (GSIDE, slots))

    zero = jnp.zeros((GSIDE, slots), bf16)
    here = col == full(1)
    after = col == full(1) + jnp.ones((), bf16)
    upper = jnp.where(here, full(2), jnp.where(after, full(3), zero))
    lower = jnp.where(here, full(4), jnp.where(after, full(5), zero))
    return full(0), upper, lower


def weight_rows(row, upper, lower, count):
    zero = jnp.zeros_like(upper)
    for a in range(count):
        yield a, jnp.where(row == float(a), upper, jnp.where(row == float(a - 1), lower, zero))


def forward_kernel(
    info_ref, grid_ref, first_t_ref, second_t_ref,
    features_ref, hidden_ref, slope_ref, decoded_ref, weights_ref,
):
    row, upper, lower = sample_columns(info_ref[...])
    for a, piece in weight_rows(row, upper, lower, GSIDE):
        weights_ref[pl.ds(a * GSIDE, GSIDE), :] = piece
    features = matmul(grid_ref[...], weights_ref[...]).astype(bf16)
    features_ref[...] = features
    pre_act = matmul(first_t_ref[...], features)
    gate = jax.nn.sigmoid(pre_act)
    hidden = (pre_act * gate).astype(bf16)
    hidden_ref[...] = hidden
    slope_ref[...] = gate * (1.0 + pre_act * (1.0 - gate))
    decoded_ref[...] = matmul(second_t_ref[...], hidden)[0:8]


def forward_call(info, grid_table, first_t, second_t, block=1024):
    channels, cells = grid_table.shape
    hid = first_t.shape[0]
    slots = info.shape[1]
    whole = lambda s: (0, 0)
    part = lambda s: (0, s)
    return pl.pallas_call(
        forward_kernel,
        grid=(slots // block,),
        in_specs=[
            pl.BlockSpec((16, block), part),
            pl.BlockSpec((channels, cells), whole),
            pl.BlockSpec((hid, channels), whole),
            pl.BlockSpec((16, hid), whole),
        ],
        out_specs=[
            pl.BlockSpec((channels, block), part),
            pl.BlockSpec((hid, block), part),
            pl.BlockSpec((hid, block), part),
            pl.BlockSpec((8, block), part),
        ],
        out_shape=[
            jax.ShapeDtypeStruct((channels, slots), bf16),
            jax.ShapeDtypeStruct((hid, slots), bf16),
            jax.ShapeDtypeStruct((hid, slots), f32),
            jax.ShapeDtypeStruct((8, slots), f32),
        ],
        scratch_shapes=[pltpu.VMEM((cells, block), bf16)],
        compiler_params=pltpu.CompilerParams(vmem_limit_bytes=VMEM_BYTES),
    )(info, grid_table, first_t, second_t)


def shade_kernel(tile_ref, rank_ref, back_ref, targets_ref, send_ref, *, tiles, capacity):
    tile = tile_ref[...]
    samples = tile.shape[1]
    rays = targets_ref.shape[1]
    members = (row_iota((tiles, samples), 0) == tile).astype(f32)
    at_rank = row_iota((capacity, samples), 0) == rank_ref[...].astype(jnp.int32)
    decoded = []
    for number in range(4):
        spread = matmul(back_ref[number], members, ((0,), (0,)), HIGHEST)
        decoded.append(jnp.sum(jnp.where(at_rank, spread, 0.0), axis=0, keepdims=True))
    raw = decoded[0]
    ray_of = row_iota((rays, samples), 1) // (MARCH + 1) == row_iota((rays, samples), 0)
    first = row_iota((rays, samples), 1) == row_iota((rays, samples), 0) * (MARCH + 1)
    on_march = jnp.where(ray_of & ~first, 1.0, 0.0)
    on_surface = jnp.where(first, 1.0, 0.0)
    density = jnp.maximum(raw, 0.0) + jnp.log1p(jnp.exp(-jnp.abs(raw)))
    along_rays = ((1,), (1,))
    total = matmul(jnp.broadcast_to(density, (8, samples)), on_march, along_rays, HIGHEST)[0:1]
    colours = jnp.concatenate(decoded[1:] + [jnp.zeros((5, samples), f32)], axis=0)
    surface = matmul(colours, on_surface, along_rays, HIGHEST)
    transmit = jnp.exp(-march_step * total)
    lighting = ambient + (1.0 - ambient) * transmit
    albedo = jax.nn.sigmoid(surface[0:3])
    errors = albedo * lighting - targets_ref[...]
    surface_grad = errors * lighting * albedo * (1.0 - albedo)
    transmit_grad = (1.0 - ambient) * jnp.sum(errors * albedo, axis=0, keepdims=True)
    march_grad = -march_step * transmit * transmit_grad
    march_all = matmul(jnp.broadcast_to(march_grad, (8, rays)), on_march, precision=HIGHEST)[0:1]
    surface_all = matmul(
        jnp.concatenate([surface_grad, jnp.zeros((5, rays), f32)], axis=0),
        on_surface,
        precision=HIGHEST,
    )
    grads = [march_all * jax.nn.sigmoid(raw)] + [surface_all[k : k + 1] for k in range(3)]
    for number in range(4):
        placed = jnp.where(at_rank, grads[number], 0.0)
        send_ref[number] = matmul(members, placed, along_rays, HIGHEST)


def backward_kernel(
    grads_ref, hidden_ref, slope_ref, features_ref, first_ref, second_ref,
    feature_grad_ref, grad_first_ref, grad_second_ref,
):
    @pl.when(pl.program_id(0) == 0)
    def _():
        grad_first_ref[...] = jnp.zeros_like(grad_first_ref)
        grad_second_ref[...] = jnp.zeros_like(grad_second_ref)

    grads = grads_ref[...]
    high = grads.astype(bf16).astype(f32)
    rest = grads - high
    mid = rest.astype(bf16).astype(f32)
    low = rest - mid
    pieces = jnp.concatenate([high, mid, low], axis=0).astype(bf16)
    pre_grad = (matmul(second_ref[...], pieces) * slope_ref[...]).astype(bf16)
    feature_grad_ref[...] = matmul(first_ref[...], pre_grad).astype(bf16)
    grad_first_ref[...] += matmul(features_ref[...], pre_grad, ((1,), (1,)))
    three = matmul(pieces, hidden_ref[...], ((1,), (1,)))
    grad_second_ref[...] += three[0:8] + three[8:16] + three[16:24]


def backward_call(grads, hidden, slope, features, first, second, block=1024):
    hid, slots = hidden.shape
    channels = features.shape[0]
    whole = lambda s: (0, 0)
    part = lambda s: (0, s)
    return pl.pallas_call(
        backward_kernel,
        grid=(slots // block,),
        in_specs=[
            pl.BlockSpec((8, block), part),
            pl.BlockSpec((hid, block), part),
            pl.BlockSpec((hid, block), part),
            pl.BlockSpec((channels, block), part),
            pl.BlockSpec((channels, hid), whole),
            pl.BlockSpec((hid, 24), whole),
        ],
        out_specs=[
            pl.BlockSpec((channels, block), part),
            pl.BlockSpec((channels, hid), whole),
            pl.BlockSpec((8, hid), whole),
        ],
        out_shape=[
            jax.ShapeDtypeStruct((channels, slots), bf16),
            jax.ShapeDtypeStruct((channels, hid), f32),
            jax.ShapeDtypeStruct((8, hid), f32),
        ],
        compiler_params=pltpu.CompilerParams(vmem_limit_bytes=VMEM_BYTES),
    )(grads, hidden, slope, features, first, second)


def spread_kernel(info_ref, grads_ref, out_ref, weights_ref, *, cell_block, slot_block):
    rows = cell_block // GSIDE
    start = jnp.full((1, 1), pl.program_id(0) * rows, jnp.int32).astype(f32).astype(bf16)
    for s in range(0, info_ref.shape[1], slot_block):
        row, upper, lower = sample_columns(info_ref[:, s : s + slot_block])
        for a, piece in weight_rows(row - start, upper, lower, rows):
            weights_ref[pl.ds(a * GSIDE, GSIDE), s : s + slot_block] = piece
    out_ref[...] = matmul(grads_ref[...], weights_ref[...], ((1,), (1,)))


def spread_call(info, grads, cells, cell_block=1024, slot_block=512):
    channels, slots = grads.shape
    whole = lambda s: (0, 0)
    return pl.pallas_call(
        functools.partial(spread_kernel, cell_block=cell_block, slot_block=slot_block),
        grid=(cells // cell_block,),
        in_specs=[pl.BlockSpec((16, slots), whole), pl.BlockSpec((channels, slots), whole)],
        out_specs=pl.BlockSpec((channels, cell_block), lambda s: (0, s)),
        out_shape=jax.ShapeDtypeStruct((channels, cells), f32),
        scratch_shapes=[pltpu.VMEM((cell_block, slots), bf16)],
        compiler_params=pltpu.CompilerParams(vmem_limit_bytes=VMEM_BYTES),
    )(info, grads)


def over_tile(x):
    return lax.all_to_all(x, "tile", split_axis=0, concat_axis=0, tiled=True)


def to_peers(x):
    fields, peers, capacity = x.shape
    return over_tile(x.transpose(1, 0, 2).reshape(peers, fields * capacity))


def from_peers(x, fields):
    peers = x.shape[0]
    return x.reshape(peers, fields, x.shape[1] // fields).transpose(1, 0, 2)


def all_sum(grad_first, grad_second):
    owners = lax.axis_size("tile")
    groups = lax.axis_size("dp")
    flat_first = grad_first.reshape(owners, -1)
    width = flat_first.shape[1]
    flat = jnp.concatenate([flat_first, grad_second.reshape(owners, -1)], axis=1)
    mine = jnp.sum(over_tile(flat), axis=0, keepdims=True)
    copies = jnp.broadcast_to(mine, (groups, mine.shape[1]))
    shared = lax.all_to_all(copies, "dp", split_axis=0, concat_axis=0, tiled=True)
    summed = jnp.sum(shared, axis=0, keepdims=True)
    everything = over_tile(jnp.broadcast_to(summed, (owners, summed.shape[1])))
    first = everything[:, :width].reshape(grad_first.shape)
    second = everything[:, width:].reshape(grad_second.shape)
    return first, second.T


def body(tile_ids, corners, offsets, targets, grid, w_first, w_second):
    owners = lax.axis_size("tile")
    samples = tile_ids.shape[0]
    capacity = 4 * samples // owners
    slot_count = owners * capacity
    cells = grid.shape[1]
    hid = w_first.shape[1]
    tile_row = tile_ids.reshape(1, samples)
    grid_table = lax.all_gather(grid, "dp", axis=0, tiled=True)

    send_info, rank = pl.pallas_call(
        functools.partial(slot_kernel, tiles=owners, capacity=capacity),
        out_shape=[
            jax.ShapeDtypeStruct((FIELDS, owners, capacity), bf16),
            jax.ShapeDtypeStruct((1, samples), f32),
        ],
    )(tile_row, corners, offsets)
    info = from_peers(to_peers(send_info), FIELDS).reshape(FIELDS, slot_count)
    info = jnp.pad(info, ((0, 16 - FIELDS), (0, 0)))

    first_t = w_first.T
    second_8 = jnp.pad(w_second, ((0, 0), (0, 4)))
    features, hidden, slope, decoded = forward_call(
        info, grid_table, first_t, jnp.pad(second_8, ((0, 0), (0, 8))).T
    )

    back = from_peers(to_peers(decoded[0:4].reshape(4, owners, capacity)), 4)
    send_grads = pl.pallas_call(
        functools.partial(shade_kernel, tiles=owners, capacity=capacity),
        out_shape=jax.ShapeDtypeStruct((4, owners, capacity), f32),
    )(tile_row, rank, back, targets)
    grads = from_peers(to_peers(send_grads), 4).reshape(4, slot_count)
    grads = jnp.pad(grads, ((0, 4), (0, 0)))

    second_24 = jnp.concatenate([second_8] * 3, axis=1)
    feature_grad, grad_first, grad_second = backward_call(
        grads, hidden, slope, features, w_first, second_24
    )
    full_grad = spread_call(info, feature_grad, cells)
    grid_grad = lax.psum_scatter(full_grad, "dp", scatter_dimension=0, tiled=True)
    grad_first, grad_second = all_sum(grad_first, grad_second[0:4])
    return (grid_grad, grad_first, grad_second)


def solution(mesh):
    in_specs = (
        P(("tile", "dp"), None),
        P(None, ("tile", "dp")),
        P(None, ("tile", "dp")),
        P(None, ("tile", "dp")),
        P("dp", "tile"),
        P(),
        P(),
    )
    out_specs = (P("dp", "tile"), P(), P())
    return jax.shard_map(body, mesh=mesh, in_specs=in_specs, out_specs=out_specs, check_vma=False)
```

```python
import functools

import jax
import jax.numpy as jnp
from jax import lax
from jax.experimental import pallas as pl
from jax.experimental.pallas import tpu as pltpu
from jax.sharding import PartitionSpec as P

GSIDE = 64
MARCH = 15
march_step = 0.1
ambient = 0.3

bf16 = jnp.bfloat16
f32 = jnp.float32
HIGHEST = lax.Precision.HIGHEST
FIELDS = 6
VMEM_BYTES = 56 << 20
SMALL_VMEM_BYTES = 12 << 20


def matmul(a, b, dims=((1,), (0,)), precision=None):
    return lax.dot_general(a, b, (dims, ((), ())), precision=precision, preferred_element_type=f32)


def row_iota(shape, dim):
    return lax.broadcasted_iota(jnp.int32, shape, dim)


def slot_kernel(tile_ref, corners_ref, offsets_ref, send_ref, rank_ref, *, tiles, capacity):
    tile = tile_ref[...]
    samples = tile.shape[1]
    members = row_iota((tiles, samples), 0) == tile
    member_rows = members.astype(f32).astype(bf16)
    before = (
        row_iota((samples, samples), 0) < row_iota((samples, samples), 1)
    ).astype(f32).astype(bf16)
    earlier = matmul(member_rows, before)
    rank = jnp.sum(jnp.where(members, earlier, 0.0), axis=0, keepdims=True)
    rank_ref[...] = rank
    at_rank = row_iota((capacity, samples), 0) == rank.astype(jnp.int32)
    along = offsets_ref[0:1]
    across = offsets_ref[1:2]
    fields = [
        corners_ref[0:1].astype(f32),
        corners_ref[1:2].astype(f32),
        (1.0 - along) * (1.0 - across),
        (1.0 - along) * across,
        along * (1.0 - across),
        along * across,
    ]
    for pair in range(FIELDS // 2):
        placed = jnp.concatenate(
            [jnp.where(at_rank, field, 0.0) for field in fields[2 * pair : 2 * pair + 2]], axis=0
        )
        send_ref[:, pair, :] = matmul(member_rows, placed.astype(bf16), ((1,), (1,)))
    send_ref[:, FIELDS // 2, :] = jnp.zeros((tiles, 2 * capacity), f32)


def sample_columns(info):
    slots = info.shape[1]
    col = row_iota((GSIDE, slots), 0).astype(f32).astype(bf16)

    def full(number):
        return jnp.broadcast_to(info[number : number + 1], (GSIDE, slots))

    zero = jnp.zeros((GSIDE, slots), bf16)
    here = col == full(1)
    after = col == full(1) + jnp.ones((), bf16)
    upper = jnp.where(here, full(2), jnp.where(after, full(3), zero))
    lower = jnp.where(here, full(4), jnp.where(after, full(5), zero))
    return full(0), upper, lower


def weight_rows(row, upper, lower, count):
    zero = jnp.zeros_like(upper)
    for a in range(count):
        yield a, jnp.where(row == float(a), upper, jnp.where(row == float(a - 1), lower, zero))


def logistic(x):
    return 0.5 + 0.5 * jnp.tanh(0.5 * x)


def forward_kernel(
    info_ref, grid_ref, first_t_ref, second_t_ref, features_ref, decoded_ref, weights_ref, *, rows
):
    row, upper, lower = sample_columns(info_ref[...].astype(bf16))
    cells = rows * GSIDE
    total = None
    for first_row in range(0, GSIDE, rows):
        here = pl.ds(first_row * GSIDE, cells)
        for a, piece in weight_rows(row - float(first_row), upper, lower, rows):
            weights_ref[pl.ds((first_row + a) * GSIDE, GSIDE), :] = piece
        term = matmul(grid_ref[:, here], weights_ref[here, :])
        total = term if total is None else total + term
    features = total.astype(bf16)
    features_ref[...] = features
    pre_act = matmul(first_t_ref[...], features)
    hidden = (pre_act * logistic(pre_act)).astype(bf16)
    decoded_ref[...] = matmul(second_t_ref[...], hidden)[0:4]


def forward_call(info, grid_table, first_t, second_t, block=1024, rows=8):
    channels, cells = grid_table.shape
    hid = first_t.shape[0]
    slots = info.shape[1]
    whole = lambda s: (0, 0)
    part = lambda s: (0, s)
    return pl.pallas_call(
        functools.partial(forward_kernel, rows=rows),
        grid=(slots // block,),
        in_specs=[
            pl.BlockSpec((8, block), part),
            pl.BlockSpec((channels, cells), whole),
            pl.BlockSpec((hid, channels), whole),
            pl.BlockSpec((16, hid), whole),
        ],
        out_specs=[pl.BlockSpec((channels, block), part), pl.BlockSpec((4, block), part)],
        out_shape=[
            jax.ShapeDtypeStruct((channels, slots), bf16),
            jax.ShapeDtypeStruct((4, slots), f32),
        ],
        scratch_shapes=[pltpu.VMEM((cells, block), bf16)],
        compiler_params=pltpu.CompilerParams(vmem_limit_bytes=VMEM_BYTES),
    )(info, grid_table, first_t, second_t)


def shade_kernel(tile_ref, rank_ref, back_ref, targets_ref, send_ref, *, tiles, capacity):
    tile = tile_ref[...]
    samples = tile.shape[1]
    rays = targets_ref.shape[1]
    members = (row_iota((tiles, samples), 0) == tile).astype(f32)
    at_rank = row_iota((capacity, samples), 0) == rank_ref[...].astype(jnp.int32)
    decoded = []
    for number in range(4):
        spread = matmul(
            back_ref[:, number * capacity : (number + 1) * capacity], members, ((0,), (0,)), HIGHEST
        )
        decoded.append(jnp.sum(jnp.where(at_rank, spread, 0.0), axis=0, keepdims=True))
    raw = decoded[0]
    ray_of = row_iota((rays, samples), 1) // (MARCH + 1) == row_iota((rays, samples), 0)
    first = row_iota((rays, samples), 1) == row_iota((rays, samples), 0) * (MARCH + 1)
    on_march = jnp.where(ray_of & ~first, 1.0, 0.0)
    on_surface = jnp.where(first, 1.0, 0.0)
    density = jnp.maximum(raw, 0.0) + jnp.log1p(jnp.exp(-jnp.abs(raw)))
    along_rays = ((1,), (1,))
    total = matmul(jnp.broadcast_to(density, (8, samples)), on_march, along_rays, HIGHEST)[0:1]
    colours = jnp.concatenate(decoded[1:] + [jnp.zeros((5, samples), f32)], axis=0)
    surface = matmul(colours, on_surface, along_rays, HIGHEST)
    transmit = jnp.exp(-march_step * total)
    lighting = ambient + (1.0 - ambient) * transmit
    albedo = jax.nn.sigmoid(surface[0:3])
    errors = albedo * lighting - targets_ref[...]
    surface_grad = errors * lighting * albedo * (1.0 - albedo)
    transmit_grad = (1.0 - ambient) * jnp.sum(errors * albedo, axis=0, keepdims=True)
    march_grad = -march_step * transmit * transmit_grad
    march_all = matmul(jnp.broadcast_to(march_grad, (8, rays)), on_march, precision=HIGHEST)[0:1]
    surface_all = matmul(
        jnp.concatenate([surface_grad, jnp.zeros((5, rays), f32)], axis=0),
        on_surface,
        precision=HIGHEST,
    )
    grads = [march_all * jax.nn.sigmoid(raw)] + [surface_all[k : k + 1] for k in range(3)]
    for number in range(4):
        placed = jnp.where(at_rank, grads[number], 0.0)
        send_ref[:, number * capacity : (number + 1) * capacity] = matmul(
            members, placed, along_rays, HIGHEST
        )


def exact_pieces(grads):
    grads = jnp.concatenate([grads, jnp.zeros_like(grads)], axis=0)
    high = grads.astype(bf16).astype(f32)
    rest = grads - high
    mid = rest.astype(bf16).astype(f32)
    return jnp.concatenate([high, mid, rest - mid], axis=0).astype(bf16)


def exact_pieces(grads):
    grads = jnp.concatenate([grads, jnp.zeros_like(grads)], axis=0)
    high = grads.astype(bf16).astype(f32)
    rest = grads - high
    mid = rest.astype(bf16).astype(f32)
    return jnp.concatenate([high, mid, rest - mid], axis=0).astype(bf16)


def backward_kernel(
    grads_ref, features_ref, first_t_ref, first_ref, second_ref,
    feature_grad_ref, grad_first_ref, grad_second_ref, first_sum, second_sum,
):
    @pl.when(pl.program_id(0) == 0)
    def _():
        first_sum[...] = jnp.zeros_like(first_sum)
        second_sum[...] = jnp.zeros_like(second_sum)

    features = features_ref[...]
    pre_act = matmul(first_t_ref[...], features)
    gate = logistic(pre_act)
    hidden = (pre_act * gate).astype(bf16)
    pieces = exact_pieces(grads_ref[...])
    hidden_grad = matmul(second_ref[...], pieces)
    pre_grad = (hidden_grad * gate * (1.0 + pre_act * (1.0 - gate))).astype(bf16)
    feature_grad_ref[...] = matmul(first_ref[...], pre_grad).astype(bf16)
    first_sum[...] += matmul(features, pre_grad, ((1,), (1,)))
    second_sum[...] += matmul(pieces, hidden, ((1,), (1,)))

    @pl.when(pl.program_id(0) == pl.num_programs(0) - 1)
    def _():
        grad_first_ref[...] = first_sum[...].astype(bf16)
        grad_second_ref[...] = (second_sum[0:8] + second_sum[8:16] + second_sum[16:24])[0:4]


def backward_call(grads, features, first_t, first, second, block=1024):
    hid, channels = first_t.shape
    slots = grads.shape[1]
    whole = lambda s: (0, 0)
    part = lambda s: (0, s)
    return pl.pallas_call(
        backward_kernel,
        grid=(slots // block,),
        in_specs=[
            pl.BlockSpec((4, block), part),
            pl.BlockSpec((channels, block), part),
            pl.BlockSpec((hid, channels), whole),
            pl.BlockSpec((channels, hid), whole),
            pl.BlockSpec((hid, 24), whole),
        ],
        out_specs=[
            pl.BlockSpec((channels, block), part),
            pl.BlockSpec((channels, hid), whole),
            pl.BlockSpec((4, hid), whole),
        ],
        out_shape=[
            jax.ShapeDtypeStruct((channels, slots), bf16),
            jax.ShapeDtypeStruct((channels, hid), bf16),
            jax.ShapeDtypeStruct((4, hid), f32),
        ],
        scratch_shapes=[pltpu.VMEM((channels, hid), f32), pltpu.VMEM((24, hid), f32)],
        compiler_params=pltpu.CompilerParams(vmem_limit_bytes=VMEM_BYTES),
    )(grads, features, first_t, first, second)


def spread_kernel(info_ref, grads_ref, out_ref, weights_ref, *, slot_block):
    rows = out_ref.shape[1] // GSIDE
    start = jnp.full((1, 1), pl.program_id(0) * rows, jnp.int32).astype(f32).astype(bf16)
    total = None
    for s in range(0, info_ref.shape[1], slot_block):
        here = slice(s, s + slot_block)
        row, upper, lower = sample_columns(info_ref[:, here].astype(bf16))
        for a, piece in weight_rows(row - start, upper, lower, rows):
            weights_ref[pl.ds(a * GSIDE, GSIDE), here] = piece
        term = matmul(grads_ref[:, here], weights_ref[:, here], ((1,), (1,)))
        total = term if total is None else total + term
    out_ref[...] = total


def spread_call(info, grads, cells, block=1024, slot_block=512):
    channels, slots = grads.shape
    whole = lambda s: (0, 0)
    return pl.pallas_call(
        functools.partial(spread_kernel, slot_block=slot_block),
        grid=(cells // block,),
        in_specs=[pl.BlockSpec((8, slots), whole), pl.BlockSpec((channels, slots), whole)],
        out_specs=pl.BlockSpec((channels, block), lambda s: (0, s)),
        out_shape=jax.ShapeDtypeStruct((channels, cells), f32),
        scratch_shapes=[pltpu.VMEM((block, slots), bf16)],
        compiler_params=pltpu.CompilerParams(vmem_limit_bytes=VMEM_BYTES),
    )(info, grads)


def over_tile(x):
    return lax.all_to_all(x, "tile", split_axis=0, concat_axis=0, tiled=True)


def all_sum(grad_first, grad_second):
    owners = lax.axis_size("tile")
    groups = lax.axis_size("dp")
    channels, hid = grad_first.shape
    first = grad_first.reshape(owners, channels // owners, hid)
    second = grad_second.astype(bf16).reshape(4, owners, hid // owners).transpose(1, 0, 2)
    second = jnp.pad(second, ((0, 0), (0, 0), (0, 128 - hid // owners)))
    mine = jnp.sum(over_tile(jnp.concatenate([first, second], axis=2)).astype(f32), axis=0)
    copies = jnp.broadcast_to(mine, (groups,) + mine.shape)
    shared = lax.all_to_all(copies, "dp", split_axis=0, concat_axis=0, tiled=True)
    summed = jnp.sum(shared, axis=0).astype(bf16)
    everything = over_tile(jnp.broadcast_to(summed, (owners,) + summed.shape)).astype(f32)
    first = everything[:, :, :hid].reshape(channels, hid)
    second = everything[:, :, hid : hid + hid // owners].transpose(0, 2, 1).reshape(hid, 4)
    return first, second


def body(tile_ids, corners, offsets, targets, grid, w_first, w_second):
    owners = lax.axis_size("tile")
    samples = tile_ids.shape[0]
    capacity = 4 * samples // owners
    slot_count = owners * capacity
    cells = grid.shape[1]
    tile_row = tile_ids.reshape(1, samples)
    grid_table = lax.all_gather(grid, "dp", axis=0, tiled=True)

    send_info, rank = pl.pallas_call(
        functools.partial(slot_kernel, tiles=owners, capacity=capacity),
        out_shape=[
            jax.ShapeDtypeStruct((owners, FIELDS // 2 + 1, 2 * capacity), f32),
            jax.ShapeDtypeStruct((1, samples), f32),
        ],
        compiler_params=pltpu.CompilerParams(vmem_limit_bytes=SMALL_VMEM_BYTES),
    )(tile_row, corners, offsets)
    first_t = w_first.T
    second_8 = jnp.pad(w_second, ((0, 0), (0, 4)))
    second_t = jnp.pad(second_8, ((0, 0), (0, 8))).T
    info = over_tile(send_info).reshape(owners, 8, capacity).transpose(1, 0, 2)
    info = info.reshape(8, slot_count)

    features, decoded = forward_call(info, grid_table, first_t, second_t)

    back = over_tile(decoded.reshape(4, owners, capacity).transpose(1, 0, 2).reshape(owners, 2, -1))
    send_grads = pl.pallas_call(
        functools.partial(shade_kernel, tiles=owners, capacity=capacity),
        out_shape=jax.ShapeDtypeStruct((owners, 4 * capacity), f32),
        compiler_params=pltpu.CompilerParams(vmem_limit_bytes=SMALL_VMEM_BYTES),
    )(tile_row, rank, back.reshape(owners, 4 * capacity), targets)
    grads = over_tile(send_grads.reshape(owners, 2, -1))
    grads = grads.reshape(owners, 4, capacity).transpose(1, 0, 2).reshape(4, slot_count)

    second_24 = jnp.concatenate([second_8] * 3, axis=1)
    feature_grad, grad_first, grad_second = backward_call(
        grads, features, first_t, w_first, second_24
    )
    share = spread_call(info, feature_grad, cells)
    grid_grad = lax.psum_scatter(share, "dp", scatter_dimension=0, tiled=True)
    share, grad_first, grad_second = lax.optimization_barrier((share, grad_first, grad_second))
    grad_first, grad_second = all_sum(grad_first, grad_second)
    return (grid_grad, grad_first, grad_second)


def solution(mesh):
    in_specs = (
        P(("tile", "dp"), None),
        P(None, ("tile", "dp")),
        P(None, ("tile", "dp")),
        P(None, ("tile", "dp")),
        P("dp", "tile"),
        P(),
        P(),
    )
    out_specs = (P("dp", "tile"), P(), P())
    return jax.shard_map(body, mesh=mesh, in_specs=in_specs, out_specs=out_specs, check_vma=False)
```

```python
import functools

import jax
import jax.numpy as jnp
from jax import lax
from jax.experimental import pallas as pl
from jax.experimental.pallas import tpu as pltpu
from jax.sharding import PartitionSpec as P

GSIDE = 64
MARCH = 15
march_step = 0.1
ambient = 0.3

bf16 = jnp.bfloat16
f32 = jnp.float32
HIGHEST = lax.Precision.HIGHEST
FIELDS = 6
VMEM_BYTES = 56 << 20
SMALL_VMEM_BYTES = 12 << 20


def matmul(a, b, dims=((1,), (0,)), precision=None):
    return lax.dot_general(a, b, (dims, ((), ())), precision=precision, preferred_element_type=f32)


def row_iota(shape, dim):
    return lax.broadcasted_iota(jnp.int32, shape, dim)


def slot_kernel(
    tile_ref, corners_ref, offsets_ref, tile_column_ref, row_column_ref, send_ref, slot_ref,
    *, tiles, capacity,
):
    tile = tile_ref[...]
    samples = tile.shape[1]
    members = row_iota((tiles, samples), 0) == tile
    member_rows = members.astype(f32).astype(bf16)
    order = corners_ref[0:1] * samples + row_iota((1, samples), 1)
    part = 128
    rank = jnp.zeros((1, samples), f32)
    count = jnp.zeros((1, samples), f32)
    for first in range(0, samples, part):
        here = slice(first, first + part)
        same = tile_column_ref[here] == tile
        order_column = row_column_ref[here] * samples + row_iota((part, 1), 0) + first
        rank += jnp.sum(jnp.where(same & (order_column < order), 1.0, 0.0), axis=0, keepdims=True)
        count += jnp.sum(jnp.where(same, 1.0, 0.0), axis=0, keepdims=True)
    lead = jnp.full((1, samples), -float(samples), f32)
    for first in range(0, samples, part):
        here = slice(first, first + part)
        same = tile_column_ref[here] == tile
        row_column = row_column_ref[here]
        order_column = row_column * samples + row_iota((part, 1), 0) + first
        rank_column = jnp.sum(
            jnp.where(same & (order < order_column), 1.0, 0.0), axis=1, keepdims=True
        )
        ahead = jnp.where(same & (order_column <= order), row_column.astype(f32) - rank_column, -1e4)
        lead = jnp.maximum(lead, jnp.max(ahead, axis=0, keepdims=True))
    slot = rank + jnp.minimum(lead, float(capacity) - count)
    slot_ref[...] = slot
    at_slot = row_iota((capacity, samples), 0) == slot.astype(jnp.int32)
    along = offsets_ref[0:1]
    across = offsets_ref[1:2]
    fields = [
        corners_ref[0:1].astype(f32),
        corners_ref[1:2].astype(f32),
        (1.0 - along) * (1.0 - across),
        (1.0 - along) * across,
        along * (1.0 - across),
        along * across,
    ]
    for pair in range(FIELDS // 2):
        placed = jnp.concatenate(
            [jnp.where(at_slot, field, 0.0) for field in fields[2 * pair : 2 * pair + 2]], axis=0
        )
        send_ref[:, pair, :] = matmul(member_rows, placed.astype(bf16), ((1,), (1,)))
    send_ref[:, FIELDS // 2, :] = jnp.zeros((tiles, 2 * capacity), f32)


def sample_columns(info):
    slots = info.shape[1]
    col = row_iota((GSIDE, slots), 0).astype(f32).astype(bf16)

    def full(number):
        return jnp.broadcast_to(info[number : number + 1], (GSIDE, slots))

    zero = jnp.zeros((GSIDE, slots), bf16)
    here = col == full(1)
    after = col == full(1) + jnp.ones((), bf16)
    upper = jnp.where(here, full(2), jnp.where(after, full(3), zero))
    lower = jnp.where(here, full(4), jnp.where(after, full(5), zero))
    return full(0), upper, lower


def weight_rows(row, upper, lower, count):
    zero = jnp.zeros_like(upper)
    for a in range(count):
        yield a, jnp.where(row == float(a), upper, jnp.where(row == float(a - 1), lower, zero))


def logistic(x):
    return 0.5 + 0.5 * jnp.tanh(0.5 * x)


WINDOWS = (16, 24, 32, 40, GSIDE)
ALIGN = 4


def in_window(least, most, run):
    begin = jnp.minimum(jnp.maximum(least, 0), GSIDE - 1) // ALIGN * ALIGN
    need = most + 1 - begin
    smaller = -GSIDE
    for size in WINDOWS:
        fits = need <= size if size < GSIDE else need > smaller

        @pl.when((need > smaller) & fits)
        def _(size=size):
            run(jnp.minimum(begin, GSIDE - size), size)

        smaller = size


def window_bounds(info, block):
    slots = info.shape[1]
    filled = jnp.sum(info[2:6], axis=0) > 0.0
    row = info[0].astype(jnp.int32)
    by_block = lambda x: x.reshape(slots // block, block)
    least = jnp.min(by_block(jnp.where(filled, row, GSIDE - 1)), axis=1)
    most = jnp.max(by_block(jnp.where(filled, row + 1, 0)), axis=1)
    number = jnp.arange(slots, dtype=jnp.int32) // (slots // GSIDE)
    group = jnp.arange(0, GSIDE, block * GSIDE // slots, dtype=jnp.int32)[:, None]
    touches = filled & (row + 1 >= group) & (row < group + block * GSIDE // slots)
    first = jnp.min(jnp.where(touches, number, GSIDE - 1), axis=1)
    last = jnp.max(jnp.where(touches, number, 0), axis=1)
    return jnp.stack([least, most, first, last])


def small(value):
    return jnp.full((1, 1), value, jnp.int32).astype(f32).astype(bf16)


def forward_kernel(
    bounds_ref, info_ref, grid_ref, first_t_ref, second_t_ref,
    features_ref, decoded_ref, weights_ref, *, rows,
):
    row, upper, lower = sample_columns(info_ref[...].astype(bf16))

    def gather(start, size):
        local = row - small(start)
        total = None
        for first_row in range(0, size, rows):
            here = pl.ds(first_row * GSIDE, rows * GSIDE)
            for a, piece in weight_rows(local - float(first_row), upper, lower, rows):
                weights_ref[pl.ds((first_row + a) * GSIDE, GSIDE), :] = piece
            there = pl.multiple_of((start + first_row) * GSIDE, ALIGN * GSIDE)
            term = matmul(grid_ref[:, pl.ds(there, rows * GSIDE)], weights_ref[here, :])
            total = term if total is None else total + term
        features_ref[...] = total.astype(bf16)

    step = pl.program_id(0)
    in_window(bounds_ref[0, step], bounds_ref[1, step], gather)
    pre_act = matmul(first_t_ref[...], features_ref[...])
    hidden = (pre_act * logistic(pre_act)).astype(bf16)
    decoded_ref[...] = matmul(second_t_ref[...], hidden)[0:4]


def forward_call(bounds, info, grid_table, first_t, second_t, block, rows=8):
    channels, cells = grid_table.shape
    hid = first_t.shape[0]
    slots = info.shape[1]
    whole = lambda s, bounds: (0, 0)
    part = lambda s, bounds: (0, s)
    return pl.pallas_call(
        functools.partial(forward_kernel, rows=rows),
        grid_spec=pltpu.PrefetchScalarGridSpec(
            num_scalar_prefetch=1,
            grid=(slots // block,),
            in_specs=[
                pl.BlockSpec((8, block), part),
                pl.BlockSpec((channels, cells), whole),
                pl.BlockSpec((hid, channels), whole),
                pl.BlockSpec((16, hid), whole),
            ],
            out_specs=[pl.BlockSpec((channels, block), part), pl.BlockSpec((4, block), part)],
            scratch_shapes=[pltpu.VMEM((cells, block), bf16)],
        ),
        out_shape=[
            jax.ShapeDtypeStruct((channels, slots), bf16),
            jax.ShapeDtypeStruct((4, slots), f32),
        ],
        compiler_params=pltpu.CompilerParams(vmem_limit_bytes=VMEM_BYTES),
    )(bounds, info, grid_table, first_t, second_t)


def shade_kernel(tile_ref, slot_ref, back_ref, targets_ref, send_ref, *, tiles, capacity):
    tile = tile_ref[...]
    samples = tile.shape[1]
    rays = targets_ref.shape[1]
    members = (row_iota((tiles, samples), 0) == tile).astype(f32)
    at_slot = row_iota((capacity, samples), 0) == slot_ref[...].astype(jnp.int32)
    decoded = []
    for number in range(4):
        spread = matmul(
            back_ref[:, number * capacity : (number + 1) * capacity], members, ((0,), (0,)), HIGHEST
        )
        decoded.append(jnp.sum(jnp.where(at_slot, spread, 0.0), axis=0, keepdims=True))
    raw = decoded[0]
    ray_of = row_iota((rays, samples), 1) // (MARCH + 1) == row_iota((rays, samples), 0)
    first = row_iota((rays, samples), 1) == row_iota((rays, samples), 0) * (MARCH + 1)
    on_march = jnp.where(ray_of & ~first, 1.0, 0.0)
    on_surface = jnp.where(first, 1.0, 0.0)
    density = jnp.maximum(raw, 0.0) + jnp.log1p(jnp.exp(-jnp.abs(raw)))
    along_rays = ((1,), (1,))
    total = matmul(jnp.broadcast_to(density, (8, samples)), on_march, along_rays, HIGHEST)[0:1]
    colours = jnp.concatenate(decoded[1:] + [jnp.zeros((5, samples), f32)], axis=0)
    surface = matmul(colours, on_surface, along_rays, HIGHEST)
    transmit = jnp.exp(-march_step * total)
    lighting = ambient + (1.0 - ambient) * transmit
    albedo = jax.nn.sigmoid(surface[0:3])
    errors = albedo * lighting - targets_ref[...]
    surface_grad = errors * lighting * albedo * (1.0 - albedo)
    transmit_grad = (1.0 - ambient) * jnp.sum(errors * albedo, axis=0, keepdims=True)
    march_grad = -march_step * transmit * transmit_grad
    march_all = matmul(jnp.broadcast_to(march_grad, (8, rays)), on_march, precision=HIGHEST)[0:1]
    surface_all = matmul(
        jnp.concatenate([surface_grad, jnp.zeros((5, rays), f32)], axis=0),
        on_surface,
        precision=HIGHEST,
    )
    grads = [march_all * jax.nn.sigmoid(raw)] + [surface_all[k : k + 1] for k in range(3)]
    for number in range(4):
        placed = jnp.where(at_slot, grads[number], 0.0)
        send_ref[:, number * capacity : (number + 1) * capacity] = matmul(
            members, placed, along_rays, HIGHEST
        )


def exact_pieces(grads):
    grads = jnp.concatenate([grads, jnp.zeros_like(grads)], axis=0)
    high = grads.astype(bf16).astype(f32)
    rest = grads - high
    mid = rest.astype(bf16).astype(f32)
    return jnp.concatenate([high, mid, rest - mid], axis=0).astype(bf16)


def exact_pieces(grads):
    grads = jnp.concatenate([grads, jnp.zeros_like(grads)], axis=0)
    high = grads.astype(bf16).astype(f32)
    rest = grads - high
    mid = rest.astype(bf16).astype(f32)
    return jnp.concatenate([high, mid, rest - mid], axis=0).astype(bf16)


def backward_kernel(
    grads_ref, features_ref, first_t_ref, first_ref, second_ref,
    feature_grad_ref, grad_first_ref, grad_second_ref, first_sum, second_sum,
):
    @pl.when(pl.program_id(0) == 0)
    def _():
        first_sum[...] = jnp.zeros_like(first_sum)
        second_sum[...] = jnp.zeros_like(second_sum)

    features = features_ref[...]
    pre_act = matmul(first_t_ref[...], features)
    gate = logistic(pre_act)
    hidden = (pre_act * gate).astype(bf16)
    pieces = exact_pieces(grads_ref[...])
    hidden_grad = matmul(second_ref[...], pieces)
    pre_grad = (hidden_grad * gate * (1.0 + pre_act * (1.0 - gate))).astype(bf16)
    feature_grad_ref[...] = matmul(first_ref[...], pre_grad).astype(bf16)
    first_sum[...] += matmul(features, pre_grad, ((1,), (1,)))
    second_sum[...] += matmul(pieces, hidden, ((1,), (1,)))

    @pl.when(pl.program_id(0) == pl.num_programs(0) - 1)
    def _():
        grad_first_ref[...] = first_sum[...].astype(bf16)
        grad_second_ref[...] = (second_sum[0:8] + second_sum[8:16] + second_sum[16:24])[0:4]


def backward_call(grads, features, first_t, first, second, block=1024):
    hid, channels = first_t.shape
    slots = grads.shape[1]
    whole = lambda s: (0, 0)
    part = lambda s: (0, s)
    return pl.pallas_call(
        backward_kernel,
        grid=(slots // block,),
        in_specs=[
            pl.BlockSpec((4, block), part),
            pl.BlockSpec((channels, block), part),
            pl.BlockSpec((hid, channels), whole),
            pl.BlockSpec((channels, hid), whole),
            pl.BlockSpec((hid, 24), whole),
        ],
        out_specs=[
            pl.BlockSpec((channels, block), part),
            pl.BlockSpec((channels, hid), whole),
            pl.BlockSpec((4, hid), whole),
        ],
        out_shape=[
            jax.ShapeDtypeStruct((channels, slots), bf16),
            jax.ShapeDtypeStruct((channels, hid), bf16),
            jax.ShapeDtypeStruct((4, hid), f32),
        ],
        scratch_shapes=[pltpu.VMEM((channels, hid), f32), pltpu.VMEM((24, hid), f32)],
        compiler_params=pltpu.CompilerParams(vmem_limit_bytes=VMEM_BYTES),
    )(grads, features, first_t, first, second)


def spread_kernel(bounds_ref, info_ref, grads_ref, out_ref, weights_ref, *, numbers):
    rows = out_ref.shape[1] // GSIDE
    step = pl.program_id(0)
    lanes = info_ref.shape[1] // GSIDE

    def scatter(start, size):
        total = None
        for number in range(0, size, numbers):
            there = pl.ds(
                pl.multiple_of((start + number) * lanes, ALIGN * lanes), numbers * lanes
            )
            here = slice(number * lanes, (number + numbers) * lanes)
            row, upper, lower = sample_columns(info_ref[:, there].astype(bf16))
            for a, piece in weight_rows(row - small(step * rows), upper, lower, rows):
                weights_ref[pl.ds(a * GSIDE, GSIDE), here] = piece
            term = matmul(grads_ref[:, there], weights_ref[:, here], ((1,), (1,)))
            total = term if total is None else total + term
        out_ref[...] = total

    in_window(bounds_ref[2, step], bounds_ref[3, step], scatter)


def spread_call(bounds, info, grads, cells, block, numbers=8):
    channels, slots = grads.shape
    whole = lambda s, bounds: (0, 0)
    return pl.pallas_call(
        functools.partial(spread_kernel, numbers=numbers),
        grid_spec=pltpu.PrefetchScalarGridSpec(
            num_scalar_prefetch=1,
            grid=(cells // block,),
            in_specs=[pl.BlockSpec((8, slots), whole), pl.BlockSpec((channels, slots), whole)],
            out_specs=pl.BlockSpec((channels, block), lambda s, bounds: (0, s)),
            scratch_shapes=[pltpu.VMEM((block, slots), bf16)],
        ),
        out_shape=jax.ShapeDtypeStruct((channels, cells), f32),
        compiler_params=pltpu.CompilerParams(vmem_limit_bytes=VMEM_BYTES),
    )(bounds, info, grads)


def over_tile(x):
    return lax.all_to_all(x, "tile", split_axis=0, concat_axis=0, tiled=True)


def all_sum(grad_first, grad_second):
    owners = lax.axis_size("tile")
    groups = lax.axis_size("dp")
    channels, hid = grad_first.shape
    first = grad_first.reshape(owners, channels // owners, hid)
    second = grad_second.astype(bf16).reshape(4, owners, hid // owners).transpose(1, 0, 2)
    second = jnp.pad(second, ((0, 0), (0, 0), (0, 128 - hid // owners)))
    mine = jnp.sum(over_tile(jnp.concatenate([first, second], axis=2)).astype(f32), axis=0)
    copies = jnp.broadcast_to(mine, (groups,) + mine.shape)
    shared = lax.all_to_all(copies, "dp", split_axis=0, concat_axis=0, tiled=True)
    summed = jnp.sum(shared, axis=0).astype(bf16)
    everything = over_tile(jnp.broadcast_to(summed, (owners,) + summed.shape)).astype(f32)
    first = everything[:, :, :hid].reshape(channels, hid)
    second = everything[:, :, hid : hid + hid // owners].transpose(0, 2, 1).reshape(hid, 4)
    return first, second


def body(tile_ids, corners, offsets, targets, grid, w_first, w_second):
    owners = lax.axis_size("tile")
    samples = tile_ids.shape[0]
    capacity = 4 * samples // owners
    slot_count = owners * capacity
    cells = grid.shape[1]
    tile_row = tile_ids.reshape(1, samples)
    grid_table = lax.all_gather(grid, "dp", axis=0, tiled=True)

    send_info, slot = pl.pallas_call(
        functools.partial(slot_kernel, tiles=owners, capacity=capacity),
        out_shape=[
            jax.ShapeDtypeStruct((owners, FIELDS // 2 + 1, 2 * capacity), f32),
            jax.ShapeDtypeStruct((1, samples), f32),
        ],
        compiler_params=pltpu.CompilerParams(vmem_limit_bytes=SMALL_VMEM_BYTES),
    )(tile_row, corners, offsets, tile_ids, corners[0].reshape(samples, 1))
    first_t = w_first.T
    second_8 = jnp.pad(w_second, ((0, 0), (0, 4)))
    second_t = jnp.pad(second_8, ((0, 0), (0, 8))).T
    info = over_tile(send_info).reshape(owners, 8, capacity).transpose(1, 2, 0)
    info = info.reshape(8, slot_count)
    block = 512
    bounds = window_bounds(info, block)

    features, decoded = forward_call(bounds, info, grid_table, first_t, second_t, block)

    back = over_tile(decoded.reshape(4, capacity, owners).transpose(2, 0, 1).reshape(owners, 2, -1))
    send_grads = pl.pallas_call(
        functools.partial(shade_kernel, tiles=owners, capacity=capacity),
        out_shape=jax.ShapeDtypeStruct((owners, 4 * capacity), f32),
        compiler_params=pltpu.CompilerParams(vmem_limit_bytes=SMALL_VMEM_BYTES),
    )(tile_row, slot, back.reshape(owners, 4 * capacity), targets)
    grads = over_tile(send_grads.reshape(owners, 2, -1))
    grads = grads.reshape(owners, 4, capacity).transpose(1, 2, 0).reshape(4, slot_count)

    second_24 = jnp.concatenate([second_8] * 3, axis=1)
    feature_grad, grad_first, grad_second = backward_call(
        grads, features, first_t, w_first, second_24
    )
    share = spread_call(bounds, info, feature_grad, cells, block)
    grid_grad = lax.psum_scatter(share, "dp", scatter_dimension=0, tiled=True)
    share, grad_first, grad_second = lax.optimization_barrier((share, grad_first, grad_second))
    grad_first, grad_second = all_sum(grad_first, grad_second)
    return (grid_grad, grad_first, grad_second)


def solution(mesh):
    in_specs = (
        P(("tile", "dp"), None),
        P(None, ("tile", "dp")),
        P(None, ("tile", "dp")),
        P(None, ("tile", "dp")),
        P("dp", "tile"),
        P(),
        P(),
    )
    out_specs = (P("dp", "tile"), P(), P())
    return jax.shard_map(body, mesh=mesh, in_specs=in_specs, out_specs=out_specs, check_vma=False)
```

```python
import functools

import jax
import jax.numpy as jnp
from jax import lax
from jax.experimental import pallas as pl
from jax.experimental.pallas import tpu as pltpu
from jax.sharding import PartitionSpec as P

GSIDE = 64
MARCH = 15
march_step = 0.1
ambient = 0.3

bf16 = jnp.bfloat16
f32 = jnp.float32
HIGHEST = lax.Precision.HIGHEST
FIELDS = 6
VMEM_BYTES = 40 << 20
SMALL_VMEM_BYTES = 12 << 20


def matmul(a, b, dims=((1,), (0,)), precision=None):
    return lax.dot_general(a, b, (dims, ((), ())), precision=precision, preferred_element_type=f32)


def row_iota(shape, dim):
    return lax.broadcasted_iota(jnp.int32, shape, dim)


def slot_kernel(
    tile_ref, corners_ref, offsets_ref, tile_column_ref, row_column_ref, send_ref, slot_ref,
    *, tiles, capacity,
):
    tile = tile_ref[...]
    samples = tile.shape[1]
    members = row_iota((tiles, samples), 0) == tile
    member_rows = members.astype(f32).astype(bf16)
    order = corners_ref[0:1] * samples + row_iota((1, samples), 1)
    part = 128
    rank = jnp.zeros((1, samples), f32)
    count = jnp.zeros((1, samples), f32)
    for first in range(0, samples, part):
        here = slice(first, first + part)
        same = tile_column_ref[here] == tile
        order_column = row_column_ref[here] * samples + row_iota((part, 1), 0) + first
        rank += jnp.sum(jnp.where(same & (order_column < order), 1.0, 0.0), axis=0, keepdims=True)
        count += jnp.sum(jnp.where(same, 1.0, 0.0), axis=0, keepdims=True)
    lead = jnp.full((1, samples), -float(samples), f32)
    for first in range(0, samples, part):
        here = slice(first, first + part)
        same = tile_column_ref[here] == tile
        row_column = row_column_ref[here]
        order_column = row_column * samples + row_iota((part, 1), 0) + first
        rank_column = jnp.sum(
            jnp.where(same & (order < order_column), 1.0, 0.0), axis=1, keepdims=True
        )
        ahead = jnp.where(same & (order_column <= order), row_column.astype(f32) - rank_column, -1e4)
        lead = jnp.maximum(lead, jnp.max(ahead, axis=0, keepdims=True))
    slot = rank + jnp.minimum(lead, float(capacity) - count)
    slot_ref[...] = slot
    at_slot = row_iota((capacity, samples), 0) == slot.astype(jnp.int32)
    along = offsets_ref[0:1]
    across = offsets_ref[1:2]
    fields = [
        corners_ref[0:1].astype(f32),
        corners_ref[1:2].astype(f32),
        (1.0 - along) * (1.0 - across),
        (1.0 - along) * across,
        along * (1.0 - across),
        along * across,
    ]
    for pair in range(FIELDS // 2):
        placed = jnp.concatenate(
            [jnp.where(at_slot, field, 0.0) for field in fields[2 * pair : 2 * pair + 2]], axis=0
        )
        send_ref[:, pair, :] = matmul(member_rows, placed.astype(bf16), ((1,), (1,)))
    send_ref[:, FIELDS // 2, :] = jnp.zeros((tiles, 2 * capacity), f32)


def sample_columns(info):
    slots = info.shape[1]
    col = row_iota((GSIDE, slots), 0).astype(f32).astype(bf16)

    def full(number):
        return jnp.broadcast_to(info[number : number + 1], (GSIDE, slots))

    zero = jnp.zeros((GSIDE, slots), bf16)
    here = col == full(1)
    after = col == full(1) + jnp.ones((), bf16)
    upper = jnp.where(here, full(2), jnp.where(after, full(3), zero))
    lower = jnp.where(here, full(4), jnp.where(after, full(5), zero))
    return full(0), upper, lower


def weight_rows(row, upper, lower, count):
    zero = jnp.zeros_like(upper)
    for a in range(count):
        yield a, jnp.where(row == float(a), upper, jnp.where(row == float(a - 1), lower, zero))


def logistic(x):
    return 0.5 + 0.5 * jnp.tanh(0.5 * x)


WINDOWS = (16, 24, 32, 40, GSIDE)
ALIGN = 4


def in_window(least, most, run):
    begin = jnp.minimum(jnp.maximum(least, 0), GSIDE - 1) // ALIGN * ALIGN
    need = most + 1 - begin
    smaller = -GSIDE
    for size in WINDOWS:
        fits = need <= size if size < GSIDE else need > smaller

        @pl.when((need > smaller) & fits)
        def _(size=size):
            run(jnp.minimum(begin, GSIDE - size), size)

        smaller = size


def window_bounds(info, block):
    slots = info.shape[1]
    filled = jnp.sum(info[2:6], axis=0) > 0.0
    row = info[0].astype(jnp.int32)
    by_block = lambda x: x.reshape(slots // block, block)
    least = jnp.min(by_block(jnp.where(filled, row, GSIDE - 1)), axis=1)
    most = jnp.max(by_block(jnp.where(filled, row + 1, 0)), axis=1)
    number = jnp.arange(slots, dtype=jnp.int32) // (slots // GSIDE)
    group = jnp.arange(0, GSIDE, block * GSIDE // slots, dtype=jnp.int32)[:, None]
    touches = filled & (row + 1 >= group) & (row < group + block * GSIDE // slots)
    first = jnp.min(jnp.where(touches, number, GSIDE - 1), axis=1)
    last = jnp.max(jnp.where(touches, number, 0), axis=1)
    return jnp.stack([least, most, first, last])


def small(value):
    return jnp.full((1, 1), value, jnp.int32).astype(f32).astype(bf16)


def forward_kernel(
    bounds_ref, info_ref, grid_ref, first_t_ref, second_t_ref,
    features_ref, decoded_ref, weights_ref, *, rows,
):
    row, upper, lower = sample_columns(info_ref[...].astype(bf16))

    def gather(start, size):
        local = row - small(start)
        total = None
        for first_row in range(0, size, rows):
            here = pl.ds(first_row * GSIDE, rows * GSIDE)
            for a, piece in weight_rows(local - float(first_row), upper, lower, rows):
                weights_ref[pl.ds((first_row + a) * GSIDE, GSIDE), :] = piece
            there = pl.multiple_of((start + first_row) * GSIDE, ALIGN * GSIDE)
            term = matmul(grid_ref[:, pl.ds(there, rows * GSIDE)], weights_ref[here, :])
            total = term if total is None else total + term
        features_ref[...] = total.astype(bf16)

    step = pl.program_id(0)
    in_window(bounds_ref[0, step], bounds_ref[1, step], gather)
    pre_act = matmul(first_t_ref[...], features_ref[...])
    hidden = (pre_act * logistic(pre_act)).astype(bf16)
    decoded_ref[...] = matmul(second_t_ref[...], hidden)[0:4]


def forward_call(bounds, info, grid_table, first_t, second_t, block, rows=8):
    channels, cells = grid_table.shape
    hid = first_t.shape[0]
    slots = info.shape[1]
    whole = lambda s, bounds: (0, 0)
    part = lambda s, bounds: (0, s)
    return pl.pallas_call(
        functools.partial(forward_kernel, rows=rows),
        grid_spec=pltpu.PrefetchScalarGridSpec(
            num_scalar_prefetch=1,
            grid=(slots // block,),
            in_specs=[
                pl.BlockSpec((8, block), part),
                pl.BlockSpec((channels, cells), whole),
                pl.BlockSpec((hid, channels), whole),
                pl.BlockSpec((16, hid), whole),
            ],
            out_specs=[pl.BlockSpec((channels, block), part), pl.BlockSpec((4, block), part)],
            scratch_shapes=[pltpu.VMEM((cells, block), bf16)],
        ),
        out_shape=[
            jax.ShapeDtypeStruct((channels, slots), bf16),
            jax.ShapeDtypeStruct((4, slots), f32),
        ],
        compiler_params=pltpu.CompilerParams(vmem_limit_bytes=VMEM_BYTES),
    )(bounds, info, grid_table, first_t, second_t)


def shade_kernel(tile_ref, slot_ref, back_ref, targets_ref, send_ref, *, tiles, capacity):
    tile = tile_ref[...]
    samples = tile.shape[1]
    rays = targets_ref.shape[1]
    members = (row_iota((tiles, samples), 0) == tile).astype(f32)
    at_slot = row_iota((capacity, samples), 0) == slot_ref[...].astype(jnp.int32)
    decoded = []
    for number in range(4):
        spread = matmul(
            back_ref[:, number * capacity : (number + 1) * capacity], members, ((0,), (0,)), HIGHEST
        )
        decoded.append(jnp.sum(jnp.where(at_slot, spread, 0.0), axis=0, keepdims=True))
    raw = decoded[0]
    ray_of = row_iota((rays, samples), 1) // (MARCH + 1) == row_iota((rays, samples), 0)
    first = row_iota((rays, samples), 1) == row_iota((rays, samples), 0) * (MARCH + 1)
    on_march = jnp.where(ray_of & ~first, 1.0, 0.0)
    on_surface = jnp.where(first, 1.0, 0.0)
    density = jnp.maximum(raw, 0.0) + jnp.log1p(jnp.exp(-jnp.abs(raw)))
    along_rays = ((1,), (1,))
    total = matmul(jnp.broadcast_to(density, (8, samples)), on_march, along_rays, HIGHEST)[0:1]
    colours = jnp.concatenate(decoded[1:] + [jnp.zeros((5, samples), f32)], axis=0)
    surface = matmul(colours, on_surface, along_rays, HIGHEST)
    transmit = jnp.exp(-march_step * total)
    lighting = ambient + (1.0 - ambient) * transmit
    albedo = jax.nn.sigmoid(surface[0:3])
    errors = albedo * lighting - targets_ref[...]
    surface_grad = errors * lighting * albedo * (1.0 - albedo)
    transmit_grad = (1.0 - ambient) * jnp.sum(errors * albedo, axis=0, keepdims=True)
    march_grad = -march_step * transmit * transmit_grad
    march_all = matmul(jnp.broadcast_to(march_grad, (8, rays)), on_march, precision=HIGHEST)[0:1]
    surface_all = matmul(
        jnp.concatenate([surface_grad, jnp.zeros((5, rays), f32)], axis=0),
        on_surface,
        precision=HIGHEST,
    )
    grads = [march_all * jax.nn.sigmoid(raw)] + [surface_all[k : k + 1] for k in range(3)]
    for number in range(4):
        placed = jnp.where(at_slot, grads[number], 0.0)
        send_ref[:, number * capacity : (number + 1) * capacity] = matmul(
            members, placed, along_rays, HIGHEST
        )


def exact_pieces(grads):
    grads = jnp.concatenate([grads, jnp.zeros_like(grads)], axis=0)
    high = grads.astype(bf16).astype(f32)
    rest = grads - high
    mid = rest.astype(bf16).astype(f32)
    return jnp.concatenate([high, mid, rest - mid], axis=0).astype(bf16)


def exact_pieces(grads):
    grads = jnp.concatenate([grads, jnp.zeros_like(grads)], axis=0)
    high = grads.astype(bf16).astype(f32)
    rest = grads - high
    mid = rest.astype(bf16).astype(f32)
    return jnp.concatenate([high, mid, rest - mid], axis=0).astype(bf16)


def backward_kernel(
    grads_ref, features_ref, first_t_ref, first_ref, second_ref,
    feature_grad_ref, grad_first_ref, grad_second_ref, first_sum, second_sum,
):
    @pl.when(pl.program_id(0) == 0)
    def _():
        first_sum[...] = jnp.zeros_like(first_sum)
        second_sum[...] = jnp.zeros_like(second_sum)

    features = features_ref[...]
    pre_act = matmul(first_t_ref[...], features)
    gate = logistic(pre_act)
    hidden = (pre_act * gate).astype(bf16)
    pieces = exact_pieces(grads_ref[...])
    hidden_grad = matmul(second_ref[...], pieces)
    pre_grad = (hidden_grad * gate * (1.0 + pre_act * (1.0 - gate))).astype(bf16)
    feature_grad_ref[...] = matmul(first_ref[...], pre_grad).astype(bf16)
    first_sum[...] += matmul(features, pre_grad, ((1,), (1,)))
    second_sum[...] += matmul(pieces, hidden, ((1,), (1,)))

    @pl.when(pl.program_id(0) == pl.num_programs(0) - 1)
    def _():
        grad_first_ref[...] = first_sum[...].astype(bf16)
        grad_second_ref[...] = (second_sum[0:8] + second_sum[8:16] + second_sum[16:24])[0:4]


def backward_call(grads, features, first_t, first, second, block=1024):
    hid, channels = first_t.shape
    slots = grads.shape[1]
    whole = lambda s: (0, 0)
    part = lambda s: (0, s)
    return pl.pallas_call(
        backward_kernel,
        grid=(slots // block,),
        in_specs=[
            pl.BlockSpec((4, block), part),
            pl.BlockSpec((channels, block), part),
            pl.BlockSpec((hid, channels), whole),
            pl.BlockSpec((channels, hid), whole),
            pl.BlockSpec((hid, 24), whole),
        ],
        out_specs=[
            pl.BlockSpec((channels, block), part),
            pl.BlockSpec((channels, hid), whole),
            pl.BlockSpec((4, hid), whole),
        ],
        out_shape=[
            jax.ShapeDtypeStruct((channels, slots), bf16),
            jax.ShapeDtypeStruct((channels, hid), bf16),
            jax.ShapeDtypeStruct((4, hid), f32),
        ],
        scratch_shapes=[pltpu.VMEM((channels, hid), f32), pltpu.VMEM((24, hid), f32)],
        compiler_params=pltpu.CompilerParams(vmem_limit_bytes=VMEM_BYTES),
    )(grads, features, first_t, first, second)


def spread_kernel(bounds_ref, info_ref, grads_ref, out_ref, weights_ref, *, numbers):
    rows = out_ref.shape[1] // GSIDE
    step = pl.program_id(0)
    lanes = info_ref.shape[1] // GSIDE

    def scatter(start, size):
        total = None
        for number in range(0, size, numbers):
            there = pl.ds(
                pl.multiple_of((start + number) * lanes, ALIGN * lanes), numbers * lanes
            )
            here = slice(number * lanes, (number + numbers) * lanes)
            row, upper, lower = sample_columns(info_ref[:, there].astype(bf16))
            for a, piece in weight_rows(row - small(step * rows), upper, lower, rows):
                weights_ref[pl.ds(a * GSIDE, GSIDE), here] = piece
            term = matmul(grads_ref[:, there], weights_ref[:, here], ((1,), (1,)))
            total = term if total is None else total + term
        out_ref[...] = total

    in_window(bounds_ref[2, step], bounds_ref[3, step], scatter)


def spread_call(bounds, info, grads, cells, block, numbers=8):
    channels, slots = grads.shape
    whole = lambda s, bounds: (0, 0)
    return pl.pallas_call(
        functools.partial(spread_kernel, numbers=numbers),
        grid_spec=pltpu.PrefetchScalarGridSpec(
            num_scalar_prefetch=1,
            grid=(cells // block,),
            in_specs=[pl.BlockSpec((8, slots), whole), pl.BlockSpec((channels, slots), whole)],
            out_specs=pl.BlockSpec((channels, block), lambda s, bounds: (0, s)),
            scratch_shapes=[pltpu.VMEM((block, slots), bf16)],
        ),
        out_shape=jax.ShapeDtypeStruct((channels, cells), f32),
        compiler_params=pltpu.CompilerParams(vmem_limit_bytes=VMEM_BYTES),
    )(bounds, info, grads)


def over_tile(x):
    return lax.all_to_all(x, "tile", split_axis=0, concat_axis=0, tiled=True)


def all_sum(grad_first, grad_second):
    owners = lax.axis_size("tile")
    groups = lax.axis_size("dp")
    channels, hid = grad_first.shape
    first = grad_first.reshape(owners, channels // owners, hid)
    second = grad_second.astype(bf16).reshape(4, owners, hid // owners).transpose(1, 0, 2)
    second = jnp.pad(second, ((0, 0), (0, 0), (0, 128 - hid // owners)))
    mine = jnp.sum(over_tile(jnp.concatenate([first, second], axis=2)).astype(f32), axis=0)
    copies = jnp.broadcast_to(mine, (groups,) + mine.shape)
    shared = lax.all_to_all(copies, "dp", split_axis=0, concat_axis=0, tiled=True)
    summed = jnp.sum(shared, axis=0).astype(bf16)
    everything = over_tile(jnp.broadcast_to(summed, (owners,) + summed.shape)).astype(f32)
    first = everything[:, :, :hid].reshape(channels, hid)
    second = everything[:, :, hid : hid + hid // owners].transpose(0, 2, 1).reshape(hid, 4)
    return first, second


def body(tile_ids, corners, offsets, targets, grid, w_first, w_second):
    owners = lax.axis_size("tile")
    samples = tile_ids.shape[0]
    capacity = 4 * samples // owners
    slot_count = owners * capacity
    cells = grid.shape[1]
    tile_row = tile_ids.reshape(1, samples)
    grid_table = lax.all_gather(grid, "dp", axis=0, tiled=True)

    send_info, slot = pl.pallas_call(
        functools.partial(slot_kernel, tiles=owners, capacity=capacity),
        out_shape=[
            jax.ShapeDtypeStruct((owners, FIELDS // 2 + 1, 2 * capacity), f32),
            jax.ShapeDtypeStruct((1, samples), f32),
        ],
        compiler_params=pltpu.CompilerParams(vmem_limit_bytes=SMALL_VMEM_BYTES),
    )(tile_row, corners, offsets, tile_ids, corners[0].reshape(samples, 1))
    first_t = w_first.T
    second_8 = jnp.pad(w_second, ((0, 0), (0, 4)))
    second_t = jnp.pad(second_8, ((0, 0), (0, 8))).T
    info = over_tile(send_info).reshape(owners, 8, capacity).transpose(1, 2, 0)
    info = info.reshape(8, slot_count)
    block = 1024
    bounds = window_bounds(info, block)

    features, decoded = forward_call(bounds, info, grid_table, first_t, second_t, block)

    back = over_tile(decoded.reshape(4, capacity, owners).transpose(2, 0, 1).reshape(owners, 2, -1))
    send_grads = pl.pallas_call(
        functools.partial(shade_kernel, tiles=owners, capacity=capacity),
        out_shape=jax.ShapeDtypeStruct((owners, 4 * capacity), f32),
        compiler_params=pltpu.CompilerParams(vmem_limit_bytes=SMALL_VMEM_BYTES),
    )(tile_row, slot, back.reshape(owners, 4 * capacity), targets)
    grads = over_tile(send_grads.reshape(owners, 2, -1))
    grads = grads.reshape(owners, 4, capacity).transpose(1, 2, 0).reshape(4, slot_count)

    second_24 = jnp.concatenate([second_8] * 3, axis=1)
    feature_grad, grad_first, grad_second = backward_call(
        grads, features, first_t, w_first, second_24
    )
    share = spread_call(bounds, info, feature_grad, cells, block)
    grid_grad = lax.psum_scatter(share, "dp", scatter_dimension=0, tiled=True)
    share, grad_first, grad_second = lax.optimization_barrier((share, grad_first, grad_second))
    grad_first, grad_second = all_sum(grad_first, grad_second)
    return (grid_grad, grad_first, grad_second)


def solution(mesh):
    in_specs = (
        P(("tile", "dp"), None),
        P(None, ("tile", "dp")),
        P(None, ("tile", "dp")),
        P(None, ("tile", "dp")),
        P("dp", "tile"),
        P(),
        P(),
    )
    out_specs = (P("dp", "tile"), P(), P())
    return jax.shard_map(body, mesh=mesh, in_specs=in_specs, out_specs=out_specs, check_vma=False)
```

```python
import functools

import jax
import jax.numpy as jnp
from jax import lax
from jax.experimental import pallas as pl
from jax.experimental.pallas import tpu as pltpu
from jax.sharding import PartitionSpec as P

GSIDE = 64
MARCH = 15
march_step = 0.1
ambient = 0.3

bf16 = jnp.bfloat16
f32 = jnp.float32
HIGHEST = lax.Precision.HIGHEST
FIELDS = 6
VMEM_BYTES = 40 << 20
SMALL_VMEM_BYTES = 12 << 20


def matmul(a, b, dims=((1,), (0,)), precision=None):
    return lax.dot_general(a, b, (dims, ((), ())), precision=precision, preferred_element_type=f32)


def row_iota(shape, dim):
    return lax.broadcasted_iota(jnp.int32, shape, dim)


def slot_kernel(
    tile_ref, corners_ref, offsets_ref, tile_column_ref, row_column_ref, send_ref, slot_ref,
    *, tiles, capacity,
):
    tile = tile_ref[...]
    samples = tile.shape[1]
    members = row_iota((tiles, samples), 0) == tile
    member_rows = members.astype(f32).astype(bf16)
    order = corners_ref[0:1] * samples + row_iota((1, samples), 1)
    part = 128
    rank = jnp.zeros((1, samples), f32)
    count = jnp.zeros((1, samples), f32)
    for first in range(0, samples, part):
        here = slice(first, first + part)
        same = tile_column_ref[here] == tile
        order_column = row_column_ref[here] * samples + row_iota((part, 1), 0) + first
        rank += jnp.sum(jnp.where(same & (order_column < order), 1.0, 0.0), axis=0, keepdims=True)
        count += jnp.sum(jnp.where(same, 1.0, 0.0), axis=0, keepdims=True)
    lead = jnp.full((1, samples), -float(samples), f32)
    for first in range(0, samples, part):
        here = slice(first, first + part)
        same = tile_column_ref[here] == tile
        row_column = row_column_ref[here]
        order_column = row_column * samples + row_iota((part, 1), 0) + first
        rank_column = jnp.sum(
            jnp.where(same & (order < order_column), 1.0, 0.0), axis=1, keepdims=True
        )
        ahead = jnp.where(same & (order_column <= order), row_column.astype(f32) - rank_column, -1e4)
        lead = jnp.maximum(lead, jnp.max(ahead, axis=0, keepdims=True))
    slot = rank + jnp.minimum(lead, float(capacity) - count)
    slot_ref[...] = slot
    at_slot = row_iota((capacity, samples), 0) == slot.astype(jnp.int32)
    along = offsets_ref[0:1]
    across = offsets_ref[1:2]
    fields = [
        corners_ref[0:1].astype(f32),
        corners_ref[1:2].astype(f32),
        (1.0 - along) * (1.0 - across),
        (1.0 - along) * across,
        along * (1.0 - across),
        along * across,
    ]
    for pair in range(FIELDS // 2):
        placed = jnp.concatenate(
            [jnp.where(at_slot, field, 0.0) for field in fields[2 * pair : 2 * pair + 2]], axis=0
        )
        send_ref[:, pair, :] = matmul(member_rows, placed.astype(bf16), ((1,), (1,)))
    send_ref[:, FIELDS // 2, :] = jnp.zeros((tiles, 2 * capacity), f32)


def sample_columns(info):
    slots = info.shape[1]
    col = row_iota((GSIDE, slots), 0).astype(f32).astype(bf16)

    def full(number):
        return jnp.broadcast_to(info[number : number + 1], (GSIDE, slots))

    zero = jnp.zeros((GSIDE, slots), bf16)
    here = col == full(1)
    after = col == full(1) + jnp.ones((), bf16)
    upper = jnp.where(here, full(2), jnp.where(after, full(3), zero))
    lower = jnp.where(here, full(4), jnp.where(after, full(5), zero))
    return full(0), upper, lower


def weight_rows(row, upper, lower, count):
    zero = jnp.zeros_like(upper)
    for a in range(count):
        yield a, jnp.where(row == float(a), upper, jnp.where(row == float(a - 1), lower, zero))


def logistic(x):
    return 0.5 + 0.5 * jnp.tanh(0.5 * x)


WINDOWS = (16, 24, 32, 40, GSIDE)
ALIGN = 4


def in_window(least, most, run):
    begin = jnp.minimum(jnp.maximum(least, 0), GSIDE - 1) // ALIGN * ALIGN
    need = most + 1 - begin
    smaller = -GSIDE
    for size in WINDOWS:
        fits = need <= size if size < GSIDE else need > smaller

        @pl.when((need > smaller) & fits)
        def _(size=size):
            run(jnp.minimum(begin, GSIDE - size), size)

        smaller = size


def window_bounds(info, block):
    slots = info.shape[1]
    filled = jnp.sum(info[2:6], axis=0) > 0.0
    row = info[0].astype(jnp.int32)
    by_block = lambda x: x.reshape(slots // block, block)
    least = jnp.min(by_block(jnp.where(filled, row, GSIDE - 1)), axis=1)
    most = jnp.max(by_block(jnp.where(filled, row + 1, 0)), axis=1)
    number = jnp.arange(slots, dtype=jnp.int32) // (slots // GSIDE)
    group = jnp.arange(0, GSIDE, block * GSIDE // slots, dtype=jnp.int32)[:, None]
    touches = filled & (row + 1 >= group) & (row < group + block * GSIDE // slots)
    first = jnp.min(jnp.where(touches, number, GSIDE - 1), axis=1)
    last = jnp.max(jnp.where(touches, number, 0), axis=1)
    return jnp.stack([least, most, first, last])


def small(value):
    return jnp.full((1, 1), value, jnp.int32).astype(f32).astype(bf16)


def forward_kernel(
    bounds_ref, info_ref, grid_ref, first_t_ref, second_t_ref,
    features_ref, decoded_ref, weights_ref, *, rows,
):
    row, upper, lower = sample_columns(info_ref[...].astype(bf16))

    def gather(start, size):
        local = row - small(start)
        total = None
        for first_row in range(0, size, rows):
            here = pl.ds(first_row * GSIDE, rows * GSIDE)
            for a, piece in weight_rows(local - float(first_row), upper, lower, rows):
                weights_ref[pl.ds((first_row + a) * GSIDE, GSIDE), :] = piece
            there = pl.multiple_of((start + first_row) * GSIDE, ALIGN * GSIDE)
            term = matmul(grid_ref[:, pl.ds(there, rows * GSIDE)], weights_ref[here, :])
            total = term if total is None else total + term
        features_ref[...] = total.astype(bf16)

    step = pl.program_id(0)
    in_window(bounds_ref[0, step], bounds_ref[1, step], gather)
    pre_act = matmul(first_t_ref[...], features_ref[...])
    hidden = (pre_act * logistic(pre_act)).astype(bf16)
    decoded_ref[...] = matmul(second_t_ref[...], hidden)[0:4]


def forward_call(bounds, info, grid_table, first_t, second_t, block, rows=8):
    channels, cells = grid_table.shape
    hid = first_t.shape[0]
    slots = info.shape[1]
    whole = lambda s, bounds: (0, 0)
    part = lambda s, bounds: (0, s)
    return pl.pallas_call(
        functools.partial(forward_kernel, rows=rows),
        grid_spec=pltpu.PrefetchScalarGridSpec(
            num_scalar_prefetch=1,
            grid=(slots // block,),
            in_specs=[
                pl.BlockSpec((8, block), part),
                pl.BlockSpec((channels, cells), whole),
                pl.BlockSpec((hid, channels), whole),
                pl.BlockSpec((16, hid), whole),
            ],
            out_specs=[pl.BlockSpec((channels, block), part), pl.BlockSpec((4, block), part)],
            scratch_shapes=[pltpu.VMEM((cells, block), bf16)],
        ),
        out_shape=[
            jax.ShapeDtypeStruct((channels, slots), bf16),
            jax.ShapeDtypeStruct((4, slots), f32),
        ],
        compiler_params=pltpu.CompilerParams(vmem_limit_bytes=VMEM_BYTES),
    )(bounds, info, grid_table, first_t, second_t)


def three_pieces(values):
    high = values.astype(bf16)
    rest = values - high.astype(f32)
    mid = rest.astype(bf16)
    return [high, mid, (rest - mid.astype(f32)).astype(bf16)]


def shade_kernel(tile_ref, slot_ref, back_ref, targets_ref, send_ref, *, tiles, capacity):
    tile = tile_ref[...]
    samples = tile.shape[1]
    rays = targets_ref.shape[1]
    members = (row_iota((tiles, samples), 0) == tile).astype(f32).astype(bf16)
    at_slot = row_iota((capacity, samples), 0) == slot_ref[...].astype(jnp.int32)
    spread = matmul(jnp.concatenate(three_pieces(back_ref[...].T), axis=0), members)
    width = 4 * capacity
    spread = spread[0:width] + spread[width : 2 * width] + spread[2 * width :]
    decoded = []
    for number in range(4):
        own = jnp.where(at_slot, spread[number * capacity : (number + 1) * capacity], 0.0)
        decoded.append(jnp.sum(own, axis=0, keepdims=True))
    raw = decoded[0]
    ray_of = row_iota((rays, samples), 1) // (MARCH + 1) == row_iota((rays, samples), 0)
    first = row_iota((rays, samples), 1) == row_iota((rays, samples), 0) * (MARCH + 1)
    on_march = jnp.where(ray_of & ~first, 1.0, 0.0)
    on_surface = jnp.where(first, 1.0, 0.0)
    density = jnp.maximum(raw, 0.0) + jnp.log1p(jnp.exp(-jnp.abs(raw)))
    along_rays = ((1,), (1,))
    total = matmul(jnp.broadcast_to(density, (8, samples)), on_march, along_rays, HIGHEST)[0:1]
    colours = jnp.concatenate(decoded[1:] + [jnp.zeros((5, samples), f32)], axis=0)
    surface = matmul(colours, on_surface, along_rays, HIGHEST)
    transmit = jnp.exp(-march_step * total)
    lighting = ambient + (1.0 - ambient) * transmit
    albedo = jax.nn.sigmoid(surface[0:3])
    errors = albedo * lighting - targets_ref[...]
    surface_grad = errors * lighting * albedo * (1.0 - albedo)
    transmit_grad = (1.0 - ambient) * jnp.sum(errors * albedo, axis=0, keepdims=True)
    march_grad = -march_step * transmit * transmit_grad
    march_all = matmul(jnp.broadcast_to(march_grad, (8, rays)), on_march, precision=HIGHEST)[0:1]
    surface_all = matmul(
        jnp.concatenate([surface_grad, jnp.zeros((5, rays), f32)], axis=0),
        on_surface,
        precision=HIGHEST,
    )
    grads = [march_all * jax.nn.sigmoid(raw)] + [surface_all[k : k + 1] for k in range(3)]
    for pair in range(2):
        placed = jnp.concatenate(
            [jnp.where(at_slot, grad, 0.0) for grad in grads[2 * pair : 2 * pair + 2]], axis=0
        )
        sums = [matmul(members, piece, along_rays) for piece in three_pieces(placed)]
        send_ref[:, pair, :] = sums[0] + sums[1] + sums[2]


def exact_pieces(grads):
    grads = jnp.concatenate([grads, jnp.zeros_like(grads)], axis=0)
    high = grads.astype(bf16).astype(f32)
    rest = grads - high
    mid = rest.astype(bf16).astype(f32)
    return jnp.concatenate([high, mid, rest - mid], axis=0).astype(bf16)


def exact_pieces(grads):
    grads = jnp.concatenate([grads, jnp.zeros_like(grads)], axis=0)
    high = grads.astype(bf16).astype(f32)
    rest = grads - high
    mid = rest.astype(bf16).astype(f32)
    return jnp.concatenate([high, mid, rest - mid], axis=0).astype(bf16)


def backward_kernel(
    grads_ref, features_ref, first_t_ref, first_ref, second_ref,
    feature_grad_ref, grad_first_ref, grad_second_ref, first_sum, second_sum,
):
    @pl.when(pl.program_id(0) == 0)
    def _():
        first_sum[...] = jnp.zeros_like(first_sum)
        second_sum[...] = jnp.zeros_like(second_sum)

    features = features_ref[...]
    pre_act = matmul(first_t_ref[...], features)
    gate = logistic(pre_act)
    active = pre_act * gate
    hidden = active.astype(bf16)
    pieces = exact_pieces(grads_ref[...])
    hidden_grad = matmul(second_ref[...], pieces)
    pre_grad = (hidden_grad * (gate + active * (1.0 - gate))).astype(bf16)
    feature_grad_ref[...] = matmul(first_ref[...], pre_grad).astype(bf16)
    first_sum[...] += matmul(features, pre_grad, ((1,), (1,)))
    second_sum[...] += matmul(pieces, hidden, ((1,), (1,)))

    @pl.when(pl.program_id(0) == pl.num_programs(0) - 1)
    def _():
        grad_first_ref[...] = first_sum[...].astype(bf16)
        grad_second_ref[...] = (second_sum[0:8] + second_sum[8:16] + second_sum[16:24])[0:4]


def backward_call(grads, features, first_t, first, second, block=1024):
    hid, channels = first_t.shape
    slots = grads.shape[1]
    whole = lambda s: (0, 0)
    part = lambda s: (0, s)
    return pl.pallas_call(
        backward_kernel,
        grid=(slots // block,),
        in_specs=[
            pl.BlockSpec((4, block), part),
            pl.BlockSpec((channels, block), part),
            pl.BlockSpec((hid, channels), whole),
            pl.BlockSpec((channels, hid), whole),
            pl.BlockSpec((hid, 24), whole),
        ],
        out_specs=[
            pl.BlockSpec((channels, block), part),
            pl.BlockSpec((channels, hid), whole),
            pl.BlockSpec((4, hid), whole),
        ],
        out_shape=[
            jax.ShapeDtypeStruct((channels, slots), bf16),
            jax.ShapeDtypeStruct((channels, hid), bf16),
            jax.ShapeDtypeStruct((4, hid), f32),
        ],
        scratch_shapes=[pltpu.VMEM((channels, hid), f32), pltpu.VMEM((24, hid), f32)],
        compiler_params=pltpu.CompilerParams(vmem_limit_bytes=VMEM_BYTES),
    )(grads, features, first_t, first, second)


def spread_kernel(bounds_ref, info_ref, grads_ref, out_ref, weights_ref, *, numbers):
    rows = out_ref.shape[1] // GSIDE
    step = pl.program_id(0)
    lanes = info_ref.shape[1] // GSIDE

    def scatter(start, size):
        total = None
        for number in range(0, size, numbers):
            there = pl.ds(
                pl.multiple_of((start + number) * lanes, ALIGN * lanes), numbers * lanes
            )
            here = slice(number * lanes, (number + numbers) * lanes)
            row, upper, lower = sample_columns(info_ref[:, there].astype(bf16))
            for a, piece in weight_rows(row - small(step * rows), upper, lower, rows):
                weights_ref[pl.ds(a * GSIDE, GSIDE), here] = piece
            term = matmul(grads_ref[:, there], weights_ref[:, here], ((1,), (1,)))
            total = term if total is None else total + term
        out_ref[...] = total

    in_window(bounds_ref[2, step], bounds_ref[3, step], scatter)


def spread_call(bounds, info, grads, cells, block, numbers=8):
    channels, slots = grads.shape
    whole = lambda s, bounds: (0, 0)
    return pl.pallas_call(
        functools.partial(spread_kernel, numbers=numbers),
        grid_spec=pltpu.PrefetchScalarGridSpec(
            num_scalar_prefetch=1,
            grid=(cells // block,),
            in_specs=[pl.BlockSpec((8, slots), whole), pl.BlockSpec((channels, slots), whole)],
            out_specs=pl.BlockSpec((channels, block), lambda s, bounds: (0, s)),
            scratch_shapes=[pltpu.VMEM((block, slots), bf16)],
        ),
        out_shape=pltpu.HBM((channels, cells), f32),
        compiler_params=pltpu.CompilerParams(vmem_limit_bytes=VMEM_BYTES),
    )(bounds, info, grads)


def over_tile(x):
    return lax.all_to_all(x, "tile", split_axis=0, concat_axis=0, tiled=True)


def all_sum(grad_first, grad_second):
    owners = lax.axis_size("tile")
    groups = lax.axis_size("dp")
    channels, hid = grad_first.shape
    first = grad_first.reshape(owners, channels // owners, hid)
    second = grad_second.astype(bf16).reshape(4, owners, hid // owners).transpose(1, 0, 2)
    second = jnp.pad(second, ((0, 0), (0, 0), (0, 128 - hid // owners)))
    mine = jnp.sum(over_tile(jnp.concatenate([first, second], axis=2)).astype(f32), axis=0)
    copies = jnp.broadcast_to(mine, (groups,) + mine.shape)
    shared = lax.all_to_all(copies, "dp", split_axis=0, concat_axis=0, tiled=True)
    summed = jnp.sum(shared, axis=0).astype(bf16)
    everything = over_tile(jnp.broadcast_to(summed, (owners,) + summed.shape)).astype(f32)
    first = everything[:, :, :hid].reshape(channels, hid)
    second = everything[:, :, hid : hid + hid // owners].transpose(0, 2, 1).reshape(hid, 4)
    return first, second


def body(tile_ids, corners, offsets, targets, grid, w_first, w_second):
    owners = lax.axis_size("tile")
    samples = tile_ids.shape[0]
    capacity = 4 * samples // owners
    slot_count = owners * capacity
    cells = grid.shape[1]
    tile_row = tile_ids.reshape(1, samples)
    grid_table = lax.all_gather(grid, "dp", axis=0, tiled=True)

    send_info, slot = pl.pallas_call(
        functools.partial(slot_kernel, tiles=owners, capacity=capacity),
        out_shape=[
            jax.ShapeDtypeStruct((owners, FIELDS // 2 + 1, 2 * capacity), f32),
            jax.ShapeDtypeStruct((1, samples), f32),
        ],
        compiler_params=pltpu.CompilerParams(vmem_limit_bytes=SMALL_VMEM_BYTES),
    )(tile_row, corners, offsets, tile_ids, corners[0].reshape(samples, 1))
    first_t = w_first.T
    second_8 = jnp.pad(w_second, ((0, 0), (0, 4)))
    second_t = jnp.pad(second_8, ((0, 0), (0, 8))).T
    info = over_tile(send_info).reshape(owners, 8, capacity).transpose(1, 2, 0)
    info = info.reshape(8, slot_count)
    block = 1024
    bounds = window_bounds(info, block)

    features, decoded = forward_call(bounds, info, grid_table, first_t, second_t, block)

    back = over_tile(decoded.reshape(4, capacity, owners).transpose(2, 0, 1).reshape(owners, 2, -1))
    send_grads = pl.pallas_call(
        functools.partial(shade_kernel, tiles=owners, capacity=capacity),
        out_shape=jax.ShapeDtypeStruct((owners, 2, 2 * capacity), f32),
        compiler_params=pltpu.CompilerParams(vmem_limit_bytes=SMALL_VMEM_BYTES),
    )(tile_row, slot, back.reshape(owners, 4 * capacity), targets)
    grads = over_tile(send_grads)
    grads = grads.reshape(owners, 4, capacity).transpose(1, 2, 0).reshape(4, slot_count)

    second_24 = jnp.concatenate([second_8] * 3, axis=1)
    feature_grad, grad_first, grad_second = backward_call(
        grads, features, first_t, w_first, second_24
    )
    share = spread_call(bounds, info, feature_grad, cells, block)
    grid_grad = lax.psum_scatter(share, "dp", scatter_dimension=0, tiled=True)
    share, grad_first, grad_second = lax.optimization_barrier((share, grad_first, grad_second))
    grad_first, grad_second = all_sum(grad_first, grad_second)
    return (grid_grad, grad_first, grad_second)


def solution(mesh):
    in_specs = (
        P(("tile", "dp"), None),
        P(None, ("tile", "dp")),
        P(None, ("tile", "dp")),
        P(None, ("tile", "dp")),
        P("dp", "tile"),
        P(),
        P(),
    )
    out_specs = (P("dp", "tile"), P(), P())
    return jax.shard_map(body, mesh=mesh, in_specs=in_specs, out_specs=out_specs, check_vma=False)
```

```python
import functools

import jax
import jax.numpy as jnp
from jax import lax
from jax.experimental import pallas as pl
from jax.experimental.pallas import tpu as pltpu
from jax.sharding import PartitionSpec as P

GSIDE = 64
MARCH = 15
march_step = 0.1
ambient = 0.3

bf16 = jnp.bfloat16
f32 = jnp.float32
HIGHEST = lax.Precision.HIGHEST
FIELDS = 6
VMEM_BYTES = 40 << 20
SMALL_VMEM_BYTES = 12 << 20


def matmul(a, b, dims=((1,), (0,)), precision=None):
    return lax.dot_general(a, b, (dims, ((), ())), precision=precision, preferred_element_type=f32)


def row_iota(shape, dim):
    return lax.broadcasted_iota(jnp.int32, shape, dim)


def slot_kernel(
    tile_ref, corners_ref, offsets_ref, tile_column_ref, row_column_ref, send_ref, slot_ref,
    *, tiles, capacity,
):
    tile = tile_ref[...]
    samples = tile.shape[1]
    members = row_iota((tiles, samples), 0) == tile
    member_rows = members.astype(f32).astype(bf16)
    order = corners_ref[0:1] * samples + row_iota((1, samples), 1)
    part = 128
    rank = jnp.zeros((1, samples), f32)
    count = jnp.zeros((1, samples), f32)
    for first in range(0, samples, part):
        here = slice(first, first + part)
        same = tile_column_ref[here] == tile
        order_column = row_column_ref[here] * samples + row_iota((part, 1), 0) + first
        rank += jnp.sum(jnp.where(same & (order_column < order), 1.0, 0.0), axis=0, keepdims=True)
        count += jnp.sum(jnp.where(same, 1.0, 0.0), axis=0, keepdims=True)
    lead = jnp.full((1, samples), -float(samples), f32)
    for first in range(0, samples, part):
        here = slice(first, first + part)
        same = tile_column_ref[here] == tile
        row_column = row_column_ref[here]
        order_column = row_column * samples + row_iota((part, 1), 0) + first
        rank_column = jnp.sum(
            jnp.where(same & (order < order_column), 1.0, 0.0), axis=1, keepdims=True
        )
        ahead = jnp.where(same & (order_column <= order), row_column.astype(f32) - rank_column, -1e4)
        lead = jnp.maximum(lead, jnp.max(ahead, axis=0, keepdims=True))
    slot = rank + jnp.minimum(lead, float(capacity) - count)
    slot_ref[...] = slot
    at_slot = row_iota((capacity, samples), 0) == slot.astype(jnp.int32)
    along = offsets_ref[0:1]
    across = offsets_ref[1:2]
    fields = [
        corners_ref[0:1].astype(f32),
        corners_ref[1:2].astype(f32),
        (1.0 - along) * (1.0 - across),
        (1.0 - along) * across,
        along * (1.0 - across),
        along * across,
    ]
    for pair in range(FIELDS // 2):
        placed = jnp.concatenate(
            [jnp.where(at_slot, field, 0.0) for field in fields[2 * pair : 2 * pair + 2]], axis=0
        )
        send_ref[:, pair, :] = matmul(member_rows, placed.astype(bf16), ((1,), (1,)))
    send_ref[:, FIELDS // 2, :] = jnp.zeros((tiles, 2 * capacity), f32)


def sample_columns(info):
    slots = info.shape[1]
    col = row_iota((GSIDE, slots), 0).astype(f32).astype(bf16)

    def full(number):
        return jnp.broadcast_to(info[number : number + 1], (GSIDE, slots))

    zero = jnp.zeros((GSIDE, slots), bf16)
    here = col == full(1)
    after = col == full(1) + jnp.ones((), bf16)
    upper = jnp.where(here, full(2), jnp.where(after, full(3), zero))
    lower = jnp.where(here, full(4), jnp.where(after, full(5), zero))
    return full(0), upper, lower


def weight_rows(row, upper, lower, count):
    zero = jnp.zeros_like(upper)
    for a in range(count):
        yield a, jnp.where(row == float(a), upper, jnp.where(row == float(a - 1), lower, zero))


WINDOWS = (16, 24, 32, 40, GSIDE)
ALIGN = 4


def in_window(least, most, run):
    begin = jnp.minimum(jnp.maximum(least, 0), GSIDE - 1) // ALIGN * ALIGN
    need = most + 1 - begin
    smaller = -GSIDE
    for size in WINDOWS:
        fits = need <= size if size < GSIDE else need > smaller

        @pl.when((need > smaller) & fits)
        def _(size=size):
            run(jnp.minimum(begin, GSIDE - size), size)

        smaller = size


def window_bounds(info, block):
    slots = info.shape[1]
    filled = jnp.sum(info[2:6], axis=0) > 0.0
    row = info[0].astype(jnp.int32)
    by_block = lambda x: x.reshape(slots // block, block)
    least = jnp.min(by_block(jnp.where(filled, row, GSIDE - 1)), axis=1)
    most = jnp.max(by_block(jnp.where(filled, row + 1, 0)), axis=1)
    number = jnp.arange(slots, dtype=jnp.int32) // (slots // GSIDE)
    group = jnp.arange(0, GSIDE, block * GSIDE // slots, dtype=jnp.int32)[:, None]
    touches = filled & (row + 1 >= group) & (row < group + block * GSIDE // slots)
    first = jnp.min(jnp.where(touches, number, GSIDE - 1), axis=1)
    last = jnp.max(jnp.where(touches, number, 0), axis=1)
    return jnp.stack([least, most, first, last])


def small(value):
    return jnp.full((1, 1), value, jnp.int32).astype(f32).astype(bf16)


def forward_kernel(
    bounds_ref, info_ref, grid_ref, half_first_t_ref, second_t_ref,
    features_ref, decoded_ref, weights_ref, *, rows,
):
    row, upper, lower = sample_columns(info_ref[...].astype(bf16))

    def gather(start, size):
        local = row - small(start)
        total = None
        for first_row in range(0, size, rows):
            here = pl.ds(first_row * GSIDE, rows * GSIDE)
            for a, piece in weight_rows(local - float(first_row), upper, lower, rows):
                weights_ref[pl.ds((first_row + a) * GSIDE, GSIDE), :] = piece
            there = pl.multiple_of((start + first_row) * GSIDE, ALIGN * GSIDE)
            term = matmul(grid_ref[:, pl.ds(there, rows * GSIDE)], weights_ref[here, :])
            total = term if total is None else total + term
        features_ref[...] = total.astype(bf16)

    step = pl.program_id(0)
    in_window(bounds_ref[0, step], bounds_ref[1, step], gather)
    half = matmul(half_first_t_ref[...], features_ref[...])
    hidden = (half + half * jnp.tanh(half)).astype(bf16)
    decoded_ref[...] = matmul(second_t_ref[...], hidden)[0:4]


def forward_call(bounds, info, grid_table, first_t, second_t, block, rows=8):
    channels, cells = grid_table.shape
    hid = first_t.shape[0]
    slots = info.shape[1]
    whole = lambda s, bounds: (0, 0)
    part = lambda s, bounds: (0, s)
    return pl.pallas_call(
        functools.partial(forward_kernel, rows=rows),
        grid_spec=pltpu.PrefetchScalarGridSpec(
            num_scalar_prefetch=1,
            grid=(slots // block,),
            in_specs=[
                pl.BlockSpec((8, block), part),
                pl.BlockSpec((channels, cells), whole),
                pl.BlockSpec((hid, channels), whole),
                pl.BlockSpec((16, hid), whole),
            ],
            out_specs=[pl.BlockSpec((channels, block), part), pl.BlockSpec((4, block), part)],
            scratch_shapes=[pltpu.VMEM((cells, block), bf16)],
        ),
        out_shape=[
            jax.ShapeDtypeStruct((channels, slots), bf16),
            jax.ShapeDtypeStruct((4, slots), f32),
        ],
        compiler_params=pltpu.CompilerParams(vmem_limit_bytes=VMEM_BYTES),
    )(bounds, info, grid_table, first_t, second_t)


def three_pieces(values):
    high = values.astype(bf16)
    rest = values - high.astype(f32)
    mid = rest.astype(bf16)
    return [high, mid, (rest - mid.astype(f32)).astype(bf16)]


def shade_kernel(tile_ref, slot_ref, back_ref, targets_ref, send_ref, *, tiles, capacity):
    tile = tile_ref[...]
    samples = tile.shape[1]
    rays = targets_ref.shape[1]
    members = (row_iota((tiles, samples), 0) == tile).astype(f32).astype(bf16)
    at_slot = row_iota((capacity, samples), 0) == slot_ref[...].astype(jnp.int32)
    spread = matmul(jnp.concatenate(three_pieces(back_ref[...].T), axis=0), members)
    width = 4 * capacity
    spread = spread[0:width] + spread[width : 2 * width] + spread[2 * width :]
    decoded = []
    for number in range(4):
        own = jnp.where(at_slot, spread[number * capacity : (number + 1) * capacity], 0.0)
        decoded.append(jnp.sum(own, axis=0, keepdims=True))
    raw = decoded[0]
    ray_of = row_iota((rays, samples), 1) // (MARCH + 1) == row_iota((rays, samples), 0)
    first = row_iota((rays, samples), 1) == row_iota((rays, samples), 0) * (MARCH + 1)
    on_march = jnp.where(ray_of & ~first, 1.0, 0.0)
    on_surface = jnp.where(first, 1.0, 0.0)
    density = jnp.maximum(raw, 0.0) + jnp.log1p(jnp.exp(-jnp.abs(raw)))
    along_rays = ((1,), (1,))
    total = matmul(jnp.broadcast_to(density, (8, samples)), on_march, along_rays, HIGHEST)[0:1]
    colours = jnp.concatenate(decoded[1:] + [jnp.zeros((5, samples), f32)], axis=0)
    surface = matmul(colours, on_surface, along_rays, HIGHEST)
    transmit = jnp.exp(-march_step * total)
    lighting = ambient + (1.0 - ambient) * transmit
    albedo = jax.nn.sigmoid(surface[0:3])
    errors = albedo * lighting - targets_ref[...]
    surface_grad = errors * lighting * albedo * (1.0 - albedo)
    transmit_grad = (1.0 - ambient) * jnp.sum(errors * albedo, axis=0, keepdims=True)
    march_grad = -march_step * transmit * transmit_grad
    march_all = matmul(jnp.broadcast_to(march_grad, (8, rays)), on_march, precision=HIGHEST)[0:1]
    surface_all = matmul(
        jnp.concatenate([surface_grad, jnp.zeros((5, rays), f32)], axis=0),
        on_surface,
        precision=HIGHEST,
    )
    grads = [march_all * jax.nn.sigmoid(raw)] + [surface_all[k : k + 1] for k in range(3)]
    for pair in range(2):
        placed = jnp.concatenate(
            [jnp.where(at_slot, grad, 0.0) for grad in grads[2 * pair : 2 * pair + 2]], axis=0
        )
        sums = [matmul(members, piece, along_rays) for piece in three_pieces(placed)]
        send_ref[:, pair, :] = sums[0] + sums[1] + sums[2]


def exact_pieces(grads):
    grads = jnp.concatenate([grads, jnp.zeros_like(grads)], axis=0)
    high = grads.astype(bf16).astype(f32)
    rest = grads - high
    mid = rest.astype(bf16).astype(f32)
    return jnp.concatenate([high, mid, rest - mid], axis=0).astype(bf16)


def exact_pieces(grads):
    grads = jnp.concatenate([grads, jnp.zeros_like(grads)], axis=0)
    high = grads.astype(bf16).astype(f32)
    rest = grads - high
    mid = rest.astype(bf16).astype(f32)
    return jnp.concatenate([high, mid, rest - mid], axis=0).astype(bf16)


def backward_kernel(
    grads_ref, features_ref, half_first_t_ref, first_ref, second_ref,
    feature_grad_ref, grad_first_ref, grad_second_ref, first_sum, second_sum,
):
    @pl.when(pl.program_id(0) == 0)
    def _():
        first_sum[...] = jnp.zeros_like(first_sum)
        second_sum[...] = jnp.zeros_like(second_sum)

    features = features_ref[...]
    half = matmul(half_first_t_ref[...], features)
    bend = jnp.tanh(half)
    product = half * bend
    hidden = (half + product).astype(bf16)
    pieces = exact_pieces(grads_ref[...])
    hidden_grad = matmul(second_ref[...], pieces)
    pre_grad = (hidden_grad * (0.5 + 0.5 * bend) * (1.0 + half - product)).astype(bf16)
    feature_grad_ref[...] = matmul(first_ref[...], pre_grad).astype(bf16)
    first_sum[...] += matmul(features, pre_grad, ((1,), (1,)))
    second_sum[...] += matmul(pieces, hidden, ((1,), (1,)))

    @pl.when(pl.program_id(0) == pl.num_programs(0) - 1)
    def _():
        grad_first_ref[...] = first_sum[...].astype(bf16)
        grad_second_ref[...] = (second_sum[0:8] + second_sum[8:16] + second_sum[16:24])[0:4]


def backward_call(grads, features, first_t, first, second, block=1024):
    hid, channels = first_t.shape
    slots = grads.shape[1]
    whole = lambda s: (0, 0)
    part = lambda s: (0, s)
    return pl.pallas_call(
        backward_kernel,
        grid=(slots // block,),
        in_specs=[
            pl.BlockSpec((4, block), part),
            pl.BlockSpec((channels, block), part),
            pl.BlockSpec((hid, channels), whole),
            pl.BlockSpec((channels, hid), whole),
            pl.BlockSpec((hid, 24), whole),
        ],
        out_specs=[
            pl.BlockSpec((channels, block), part),
            pl.BlockSpec((channels, hid), whole),
            pl.BlockSpec((4, hid), whole),
        ],
        out_shape=[
            jax.ShapeDtypeStruct((channels, slots), bf16),
            jax.ShapeDtypeStruct((channels, hid), bf16),
            jax.ShapeDtypeStruct((4, hid), f32),
        ],
        scratch_shapes=[pltpu.VMEM((channels, hid), f32), pltpu.VMEM((24, hid), f32)],
        compiler_params=pltpu.CompilerParams(vmem_limit_bytes=VMEM_BYTES),
    )(grads, features, first_t, first, second)


def spread_kernel(bounds_ref, info_ref, grads_ref, out_ref, weights_ref, *, numbers):
    rows = out_ref.shape[1] // GSIDE
    step = pl.program_id(0)
    lanes = info_ref.shape[1] // GSIDE

    def scatter(start, size):
        total = None
        for number in range(0, size, numbers):
            there = pl.ds(
                pl.multiple_of((start + number) * lanes, ALIGN * lanes), numbers * lanes
            )
            here = slice(number * lanes, (number + numbers) * lanes)
            row, upper, lower = sample_columns(info_ref[:, there].astype(bf16))
            for a, piece in weight_rows(row - small(step * rows), upper, lower, rows):
                weights_ref[pl.ds(a * GSIDE, GSIDE), here] = piece
            term = matmul(grads_ref[:, there], weights_ref[:, here], ((1,), (1,)))
            total = term if total is None else total + term
        out_ref[...] = total

    in_window(bounds_ref[2, step], bounds_ref[3, step], scatter)


def spread_call(bounds, info, grads, cells, block, numbers=8):
    channels, slots = grads.shape
    whole = lambda s, bounds: (0, 0)
    return pl.pallas_call(
        functools.partial(spread_kernel, numbers=numbers),
        grid_spec=pltpu.PrefetchScalarGridSpec(
            num_scalar_prefetch=1,
            grid=(cells // block,),
            in_specs=[pl.BlockSpec((8, slots), whole), pl.BlockSpec((channels, slots), whole)],
            out_specs=pl.BlockSpec((channels, block), lambda s, bounds: (0, s)),
            scratch_shapes=[pltpu.VMEM((block, slots), bf16)],
        ),
        out_shape=pltpu.HBM((channels, cells), f32),
        compiler_params=pltpu.CompilerParams(vmem_limit_bytes=VMEM_BYTES),
    )(bounds, info, grads)


def over_tile(x):
    return lax.all_to_all(x, "tile", split_axis=0, concat_axis=0, tiled=True)


def all_sum(grad_first, grad_second):
    owners = lax.axis_size("tile")
    groups = lax.axis_size("dp")
    channels, hid = grad_first.shape
    first = grad_first.reshape(owners, channels // owners, hid)
    second = grad_second.astype(bf16).reshape(4, owners, hid // owners).transpose(1, 0, 2)
    second = jnp.pad(second, ((0, 0), (0, 0), (0, 128 - hid // owners)))
    mine = jnp.sum(over_tile(jnp.concatenate([first, second], axis=2)).astype(f32), axis=0)
    copies = jnp.broadcast_to(mine, (groups,) + mine.shape)
    shared = lax.all_to_all(copies, "dp", split_axis=0, concat_axis=0, tiled=True)
    summed = jnp.sum(shared, axis=0).astype(bf16)
    everything = over_tile(jnp.broadcast_to(summed, (owners,) + summed.shape))
    first = everything[:, :, :hid].reshape(channels, hid).astype(f32)
    second = everything[:, :, hid : hid + hid // owners].transpose(0, 2, 1).reshape(hid, 4).astype(f32)
    return first, second


def body(tile_ids, corners, offsets, targets, grid, w_first, w_second):
    owners = lax.axis_size("tile")
    samples = tile_ids.shape[0]
    capacity = 4 * samples // owners
    slot_count = owners * capacity
    cells = grid.shape[1]
    tile_row = tile_ids.reshape(1, samples)
    grid_table = lax.all_gather(grid, "dp", axis=0, tiled=True)

    send_info, slot = pl.pallas_call(
        functools.partial(slot_kernel, tiles=owners, capacity=capacity),
        out_shape=[
            jax.ShapeDtypeStruct((owners, FIELDS // 2 + 1, 2 * capacity), f32),
            jax.ShapeDtypeStruct((1, samples), f32),
        ],
        compiler_params=pltpu.CompilerParams(vmem_limit_bytes=SMALL_VMEM_BYTES),
    )(tile_row, corners, offsets, tile_ids, corners[0].reshape(samples, 1))
    half_first_t = 0.5 * w_first.T
    second_8 = jnp.pad(w_second, ((0, 0), (0, 4)))
    second_t = jnp.pad(second_8, ((0, 0), (0, 8))).T
    info = over_tile(send_info).reshape(owners, 8, capacity).transpose(1, 2, 0)
    info = info.reshape(8, slot_count)
    block = 1024
    bounds = window_bounds(info, block)

    features, decoded = forward_call(bounds, info, grid_table, half_first_t, second_t, block)

    back = over_tile(decoded.reshape(4, capacity, owners).transpose(2, 0, 1).reshape(owners, 2, -1))
    send_grads = pl.pallas_call(
        functools.partial(shade_kernel, tiles=owners, capacity=capacity),
        out_shape=jax.ShapeDtypeStruct((owners, 2, 2 * capacity), f32),
        compiler_params=pltpu.CompilerParams(vmem_limit_bytes=SMALL_VMEM_BYTES),
    )(tile_row, slot, back.reshape(owners, 4 * capacity), targets)
    grads = over_tile(send_grads)
    grads = grads.reshape(owners, 4, capacity).transpose(1, 2, 0).reshape(4, slot_count)

    second_24 = jnp.concatenate([second_8] * 3, axis=1)
    feature_grad, grad_first, grad_second = backward_call(
        grads, features, half_first_t, w_first, second_24
    )
    share = spread_call(bounds, info, feature_grad, cells, block)
    grid_grad = lax.psum_scatter(share, "dp", scatter_dimension=0, tiled=True)
    share, grad_first, grad_second = lax.optimization_barrier((share, grad_first, grad_second))
    grad_first, grad_second = all_sum(grad_first, grad_second)
    return (grid_grad, grad_first, grad_second)


def solution(mesh):
    in_specs = (
        P(("tile", "dp"), None),
        P(None, ("tile", "dp")),
        P(None, ("tile", "dp")),
        P(None, ("tile", "dp")),
        P("dp", "tile"),
        P(),
        P(),
    )
    out_specs = (P("dp", "tile"), P(), P())
    return jax.shard_map(body, mesh=mesh, in_specs=in_specs, out_specs=out_specs, check_vma=False)
```
